32 devices in a mesh: ctx: 32 (over z, y, x, core), chan: 1.
Axes of the slice: x: 2, y: 2, z: 4, core: 2. Of those that a mesh axis runs over, the one named last changes fastest.
Arguments:
- features: bfloat16 [8192, 3, 8192], P('ctx', None, 'chan'), may hold values from -29 to 29
- short_taps: float32 [3, 3, 8192], P(None, None, 'chan'), may hold values from -3 to 3
- decay_rate: float32 [16, 8192], P(None, 'chan'), may hold values from 6.1035156e-05 to 0.0333333333
- residue: float32 [16, 8192], P(None, 'chan'), may hold values from -1.5 to 1.5
- skip_gain: float32 [8192], P('chan'), may hold values from -4 to 4
- norm_gain: float32 [8192], P('chan'), may hold values from 0.5 to 1.5
- contig_lengths: int32 [4], replicated, may hold values from 1 to 4096, 8192 in all
Outputs:
- normed: bfloat16 [8192, 8192], P('ctx', 'chan')
The draws below stay inside these ranges and needn't reach their ends.
Inputs may be any that keep to these rules, and one draw needn't show every extreme that they name: `contig_lengths`: the lengths sum to 8192 and the longest is exactly 4096.
All inputs are finite; a program needn't handle non-finite values.
Results may differ from the reference program's by a relative error of at most 0.0024.
Values may be sent and summed in bfloat16 or wider, within the bound.
A program may use at most 128 MiB of HBM per device.

```python
import math
import jax
import jax.numpy as jnp
import numpy as np
from jax import lax

D = 8192
ORDER = 16
NCONTIG = 4
TOKENS = 8192


def draw_features(key, part):
    key_one = jax.random.fold_in(jax.random.fold_in(key, 11), 0)
    columns = 3.0 ** (jnp.arange(D, dtype=jnp.float32) / (3.0 * D))
    values = jnp.clip(jax.random.normal(key_one, (TOKENS, 3, D), jnp.float32), -5.0, 5.0) * columns
    return values.astype(jnp.bfloat16)


def draw_decay_rate(key, part):
    key_one, key_two, key_three, key_four, key_five = jax.random.split(jax.random.fold_in(key, 23), 5)
    low_end = math.log(0.5 / TOKENS)
    mid_end = math.log(min(4.0 / TOKENS, 1.0 / 64.0))
    top_end = math.log(1.0 / 64.0)
    very_slow = jnp.exp(low_end + jax.random.uniform(key_one, (ORDER, D), jnp.float32) * (mid_end - low_end))
    middle = jnp.exp(mid_end + jax.random.uniform(key_four, (ORDER, D), jnp.float32) * (top_end - mid_end))
    slow_rate = jnp.where(jax.random.uniform(key_five, (ORDER, D), jnp.float32) < 0.5, very_slow, middle)
    fast_rate = jnp.exp(math.log(1.0 / 50.0) + jax.random.uniform(key_three, (ORDER, D), jnp.float32) * math.log(50.0 / 30.0))
    share = 0.5
    picked = jax.random.uniform(key_two, (ORDER, D), jnp.float32)
    return jnp.where(picked < share, slow_rate, fast_rate).astype(jnp.float32)


def length_profile(number_of, total, bound, skew):
    loads = [(1 << 20) // math.isqrt(rank ** skew) + 1 for rank in range(2, number_of + 1)]
    surplus, given = total - bound - (number_of - 1), [1] * (number_of - 1)
    while surplus > 0:
        candidates = [i for i in range(number_of - 1) if given[i] < bound]
        whole, left = sum([loads[i] for i in candidates]), surplus
        for i in candidates:
            extra = min(bound - given[i], max(1, left * loads[i] // whole), surplus)
            given[i] = given[i] + extra
            surplus = surplus - extra
    return np.array([bound] + given)


def uneven_parts(rng, number_of, total, most, skew):
    if number_of == 2:
        one = jax.random.randint(rng, (), max(1, total - most), min(most, total - 1) + 1)
        return jnp.stack([one, total - one])
    sizes = jnp.asarray(length_profile(number_of, total, most, skew), jnp.int32)
    twos = (number_of - 1) // 2
    giver, sink = sizes[1:1 + 2 * twos:2], sizes[2:2 + 2 * twos:2]
    margin = jnp.minimum(giver - 1, most - sink)
    passed = jax.random.randint(jax.random.fold_in(rng, 1), (twos,), 0, 1 << 20) % (margin + 1)
    sizes = sizes.at[1:1 + 2 * twos:2].set(giver - passed).at[2:2 + 2 * twos:2].set(sink + passed)
    return sizes[jax.random.permutation(jax.random.fold_in(rng, 2), number_of)]


def gaussian(key, extent, scale, bound, kind=jnp.bfloat16):
    drawn = scale * jax.random.normal(key, extent, jnp.float32)
    return jnp.clip(drawn, min=-bound, max=bound).astype(kind)


def setup_inputs(seed: int = 0) -> dict:
    keys = jax.random.split(jax.random.key(seed), 8)
    features = draw_features(jax.random.fold_in(keys[7], 71), 0)
    short_taps = gaussian(keys[1], (3, 3, D), 0.6, 3.0, jnp.float32)
    decay_rate = draw_decay_rate(jax.random.fold_in(keys[7], 71), 0)
    residue = gaussian(keys[3], (ORDER, D), 0.25, 1.5, jnp.float32)
    skip_gain = gaussian(keys[4], (D,), 1.0, 4.0, jnp.float32)
    norm_gain = jnp.clip(1.0 + 0.1 * jax.random.normal(keys[5], (D,), jnp.float32), 0.5, 1.5)
    contig_lengths = uneven_parts(keys[6], NCONTIG, TOKENS, TOKENS // 2, 1).astype(jnp.int32)
    return {"features": features, "short_taps": short_taps, "decay_rate": decay_rate, "residue": residue, "skip_gain": skip_gain, "norm_gain": norm_gain, "contig_lengths": contig_lengths}


eps_norm = 1e-05

def reference(features, short_taps, decay_rate, residue, skip_gain, norm_gain, contig_lengths):
    bounds = jnp.cumsum(contig_lengths)[:-1]
    places = jnp.arange(TOKENS, dtype=jnp.int32)
    segment = lax.optimization_barrier(jnp.sum((places[:, None] >= bounds[None, :]).astype(jnp.int32), axis=1))
    keep_one = jnp.concatenate([jnp.zeros((1,), jnp.float32), (segment[1:] == segment[:-1]).astype(jnp.float32)])
    keep_two = jnp.concatenate([jnp.zeros((2,), jnp.float32), (segment[2:] == segment[:-2]).astype(jnp.float32)])
    fade = jnp.exp(-decay_rate)
    input_scale = jnp.sqrt(1.0 - jnp.exp(-2.0 * decay_rate))

    def advance(carry, inputs):
        state, prev_one, prev_two = carry
        row_now, link_one, link_two = inputs
        current = row_now.astype(jnp.float32)
        mixed_rows = short_taps[0] * current + short_taps[1] * prev_one * link_one + short_taps[2] * prev_two * link_two
        product = mixed_rows[1] * mixed_rows[2]
        state = fade * state * link_one + input_scale * product[None, :]
        filtered = lax.optimization_barrier(jnp.sum(residue * state, axis=0))
        response = mixed_rows[0] * (filtered + skip_gain * product)
        scale_row = lax.rsqrt(jnp.mean(response * response) + eps_norm)
        return ((state, current, prev_one), (response * scale_row * norm_gain).astype(jnp.bfloat16))
    start = (jnp.zeros((ORDER, D), jnp.float32), jnp.zeros((3, D), jnp.float32), jnp.zeros((3, D), jnp.float32))
    final_carry, normed = lax.scan(advance, start, (features, keep_one, keep_two), unroll=8)
    return normed
```

```python
import functools

import jax
import jax.numpy as jnp
import numpy as np
from jax import lax
from jax.experimental import pallas as pl
from jax.experimental.pallas import tpu as pltpu
from jax.sharding import PartitionSpec as P

D = 8192
eps_norm = 1e-05
RATE_TOP = 1.0 / 30.0 * (1.0 + 1e-6)
BLOCK = 32
WIDE = 16
NEAR = 7
F32 = jnp.float32
BF16 = jnp.bfloat16


def nodes_of(count):
    angle = (2 * np.arange(count) + 1) * np.pi / (2 * count)
    return RATE_TOP / 2 * (1 - np.cos(angle))


def lagrange(rate, nodes):
    count = len(nodes)
    unit = nodes / RATE_TOP
    scaled = rate * F32(1.0 / RATE_TOP)
    gaps = [scaled - F32(u) for u in unit]
    ahead = [None] * count
    for i in range(1, count):
        ahead[i] = gaps[i - 1] if i == 1 else ahead[i - 1] * gaps[i - 1]
    weights = [None] * count
    after = None
    for i in reversed(range(count)):
        norm = F32(1.0 / np.prod([unit[i] - unit[j] for j in range(count) if j != i]))
        if after is None:
            weights[i] = ahead[i] * norm
            after = gaps[i]
        else:
            weights[i] = (after if i == 0 else ahead[i] * after) * norm
            after = after * gaps[i]
    return weights


def gather_matrix(rows):
    nodes = nodes_of(WIDE)
    index = np.arange(rows // BLOCK * WIDE)
    end = (index // WIDE + 1) * BLOCK - 1
    lag = end[:, None] - np.arange(rows)[None, :]
    return np.where(lag >= 0, np.exp(-nodes[index % WIDE][:, None] * np.maximum(lag, 0)), 0.0)


def spread_matrix(rows):
    nodes = nodes_of(WIDE)
    blocks = rows // BLOCK
    index = np.arange(blocks * WIDE)
    group = index // WIDE
    place = np.arange(rows)[:, None]
    end = np.where(group == blocks - 1, -1, (group + 1) * BLOCK - 1)[None, :]
    used = (group == blocks - 1)[None, :] | (place // BLOCK == group[None, :] + 1)
    lag = place - end
    return np.where(used, np.exp(-nodes[index % WIDE][None, :] * np.maximum(lag, 0)), 0.0)


def near_matrices(rows):
    lag = np.arange(rows)[:, None] - np.arange(rows)[None, :]
    same = (np.arange(rows)[:, None] // BLOCK == np.arange(rows)[None, :] // BLOCK) & (lag >= 0)
    return np.stack(
        [np.where(same, np.exp(-node * np.maximum(lag, 0)), 0.0) for node in nodes_of(NEAR)]
    )


def bounds_of(lengths_ref, anchor):
    total = -anchor
    bounds = []
    for i in range(lengths_ref.shape[0] - 1):
        total = total + lengths_ref[i]
        bounds.append(total)
    return bounds


def seg_of(place, bounds):
    return sum((place >= b).astype(jnp.int32) for b in bounds)


def halves(value):
    high = value.astype(BF16)
    return high, (value - high.astype(F32)).astype(BF16)


def product_of(left, right):
    return jnp.dot(left, right, preferred_element_type=F32)


def wide(column, columns):
    return jnp.concatenate([column] * (columns // column.shape[1]), axis=1)


def fill_keeps(keep_ref, bounds):
    rows = keep_ref.shape[1]
    place = lax.broadcasted_iota(jnp.int32, (rows, 128), 0)
    segment = seg_of(place, bounds)
    for i in range(2):
        keep_ref[i] = (seg_of(place - (i + 1), bounds) == segment).astype(F32)


def mix(block, edge, taps, keep_ref):
    rows, columns = block.shape
    now = block.astype(F32)
    edge = edge.astype(F32)
    row = lax.broadcasted_iota(jnp.int32, (rows, columns), 0)
    one = jnp.where(row == 0, edge[1:2], pltpu.roll(now, 1, 0))
    two = pltpu.roll(now, 2, 0)
    two = jnp.where(row == 0, edge[0:1], jnp.where(row == 1, edge[1:2], two))
    return (
        taps[0:1] * now
        + taps[1:2] * (one * wide(keep_ref[0], columns))
        + taps[2:3] * (two * wide(keep_ref[1], columns))
    )


def ends_kernel(
    lengths_ref, key_ref, value_ref, edge_ref, taps_ref, rate_ref, gather_ref, state_ref, keep_ref, matrix_ref
):
    rows = key_ref.shape[1]
    bounds = bounds_of(lengths_ref, lax.axis_index("ctx") * rows)

    @pl.when(pl.program_id(0) == 0)
    def _():
        fill_keeps(keep_ref, bounds)
        place = lax.broadcasted_iota(jnp.int32, (WIDE, rows), 1)
        same = seg_of(place, bounds) == seg_of(jnp.full((WIDE, rows), rows - 1, jnp.int32), bounds)
        high, low = halves(jnp.where(same, gather_ref[...], 0.0))
        matrix_ref[:WIDE] = high
        matrix_ref[WIDE:] = low

    product = mix(key_ref[0], edge_ref[1], taps_ref[:, 1], keep_ref) * mix(
        value_ref[0], edge_ref[2], taps_ref[:, 2], keep_ref
    )
    high, low = halves(product)
    moments = product_of(matrix_ref[...], high)
    moments = moments[:WIDE] + moments[WIDE:] + product_of(matrix_ref[:WIDE], low)
    weights = lagrange(rate_ref[...], nodes_of(WIDE))
    state = weights[0] * moments[0:1]
    for i in range(1, WIDE):
        state = state + weights[i] * moments[i : i + 1]
    state_ref[...] = state.astype(BF16)


def chain_kernel(rows, lengths_ref, local_ref, rate_ref, out_ref):
    fade = jnp.exp(-rate_ref[...] * F32(rows))
    bounds = bounds_of(lengths_ref, 0)
    state = jnp.zeros(rate_ref.shape, F32)
    for i in range(local_ref.shape[0]):
        out_ref[i] = state.astype(BF16)
        whole = seg_of(jnp.int32((i + 1) * rows - 1), bounds) == seg_of(jnp.int32(i * rows - 1), bounds)
        state = state * fade * whole.astype(F32) + local_ref[i].astype(F32)


def output_kernel(
    fused,
    lengths_ref,
    query_ref,
    key_ref,
    value_ref,
    edge_ref,
    taps_ref,
    rate_ref,
    residue_ref,
    skip_ref,
    gain_ref,
    arrived_ref,
    gather_ref,
    spread_ref,
    near_ref,
    out_ref,
    square_ref,
    keep_ref,
    gather_m,
    spread_m,
    near_m,
    held_ref,
):
    rows, columns = query_ref.shape[1:]
    phase, step = pl.program_id(0), pl.program_id(1)
    bounds = bounds_of(lengths_ref, lax.axis_index("ctx") * rows)

    @pl.when((phase == 0) & (step == 0))
    def _():
        fill_keeps(keep_ref, bounds)
        square_ref[...] = jnp.zeros_like(square_ref)
        across = lax.broadcasted_iota(jnp.int32, (rows, rows), 1)
        down = lax.broadcasted_iota(jnp.int32, (rows, rows), 0)
        count = gather_ref.shape[0]
        group = lax.broadcasted_iota(jnp.int32, (count, rows), 0) // WIDE
        same = seg_of(lax.broadcasted_iota(jnp.int32, (count, rows), 1), bounds) == seg_of(
            group * BLOCK + (BLOCK - 1), bounds
        )
        high, low = halves(jnp.where(same, gather_ref[...], 0.0))
        gather_m[:count] = high
        gather_m[count:] = low
        group = lax.broadcasted_iota(jnp.int32, (rows, count), 1) // WIDE
        end = jnp.where(group == rows // BLOCK - 1, -1, group * BLOCK + (BLOCK - 1))
        same = seg_of(lax.broadcasted_iota(jnp.int32, (rows, count), 0), bounds) == seg_of(end, bounds)
        high, low = halves(jnp.where(same, spread_ref[...], 0.0))
        spread_m[:, :count] = high
        spread_m[:, count:] = low
        same = seg_of(down, bounds) == seg_of(across, bounds)
        for i in range(NEAR):
            near_m[i] = jnp.where(same, near_ref[i].astype(F32), 0.0).astype(BF16)

    @pl.when(phase == 0)
    def _():
        query = mix(query_ref[0], edge_ref[0], taps_ref[:, 0], keep_ref)
        product = mix(key_ref[0], edge_ref[1], taps_ref[:, 1], keep_ref) * mix(
            value_ref[0], edge_ref[2], taps_ref[:, 2], keep_ref
        )
        rate = rate_ref[...]
        scale = residue_ref[...] * jnp.sqrt(1.0 - jnp.exp(-2.0 * rate))
        brought = scale * arrived_ref[...].astype(F32)
        weights = lagrange(rate, nodes_of(WIDE))
        share = jnp.concatenate([jnp.sum(w * scale, axis=0, keepdims=True) for w in weights], axis=0)
        entry = jnp.concatenate([jnp.sum(w * brought, axis=0, keepdims=True) for w in weights], axis=0)
        near = [jnp.sum(w * scale, axis=0, keepdims=True) for w in lagrange(rate, nodes_of(NEAR))]
        high, low = halves(product)
        total = skip_ref[...] * product
        for i in range(NEAR):
            total = total + near[i] * product_of(near_m[i], high)
        count = gather_ref.shape[0]
        moments = product_of(gather_m[...], high)
        moments = moments[:count] + moments[count:] + product_of(gather_m[:count], low)
        last = count - WIDE
        moments = (moments[:last].reshape(-1, WIDE, columns) * share[None]).reshape(last, columns)
        high, low = halves(jnp.concatenate([moments, entry], axis=0))
        total = total + product_of(spread_m[...], jnp.concatenate([high, high], axis=0))
        total = total + product_of(spread_m[:, :count], low)
        response = query * total
        squares = response * response
        part = squares[:, :128]
        for i in range(1, columns // 128):
            part = part + squares[:, i * 128 : (i + 1) * 128]
        square_ref[...] += part
        if fused:
            held_ref[step] = response
        else:
            out_ref[...] = response

    if fused:

        @pl.when((phase == 1) & (step == 0))
        def _():
            mean = jnp.sum(square_ref[...], axis=1, keepdims=True) / D
            square_ref[...] = jnp.broadcast_to(lax.rsqrt(mean + eps_norm), square_ref.shape)

        @pl.when(phase == 1)
        def _():
            out_ref[...] = (held_ref[step] * wide(square_ref[...], columns) * gain_ref[...]).astype(BF16)


def shards(features, short_taps, decay_rate, residue, skip_gain, norm_gain, contig_lengths):
    rows, _, channels = features.shape
    count = lax.axis_size("ctx")
    fused = lax.axis_size("chan") == 1
    poles = decay_rate.shape[0]
    planes = jnp.transpose(features, (1, 0, 2))
    columns = min(512, channels)
    steps = channels // columns
    edge = lax.ppermute(features[rows - 2 :], "ctx", [(i, i + 1) for i in range(count - 1)])
    edge = jnp.transpose(edge, (1, 0, 2))
    gather = jnp.asarray(gather_matrix(rows), F32)
    spread = jnp.asarray(spread_matrix(rows), F32)
    near = jnp.asarray(near_matrices(rows), BF16)
    smem = pl.BlockSpec(memory_space=pltpu.SMEM)

    def plane(i):
        return pl.BlockSpec((1, rows, columns), lambda j: (i, 0, j))

    ends = pl.pallas_call(
        ends_kernel,
        grid=(steps,),
        in_specs=[
            smem,
            plane(1),
            plane(2),
            pl.BlockSpec((3, 2, columns), lambda j: (0, 0, j)),
            pl.BlockSpec((3, 3, columns), lambda j: (0, 0, j)),
            pl.BlockSpec((poles, columns), lambda j: (0, j)),
            pl.BlockSpec((WIDE, rows), lambda j: (rows // BLOCK - 1, 0)),
        ],
        out_specs=pl.BlockSpec((poles, columns), lambda j: (0, j)),
        out_shape=jax.ShapeDtypeStruct((poles, channels), BF16),
        scratch_shapes=[pltpu.VMEM((2, rows, 128), F32), pltpu.VMEM((2 * WIDE, rows), BF16)],
        compiler_params=pltpu.CompilerParams(vmem_limit_bytes=40 << 20),
        name="ends",
    )(contig_lengths, planes, planes, edge, short_taps, decay_rate, gather)

    slim = channels // count
    pieces = lax.all_to_all(ends.reshape(poles, count, slim), "ctx", 1, 0, tiled=False)
    mine = lax.dynamic_slice_in_dim(decay_rate, lax.axis_index("ctx") * slim, slim, 1)
    chained = pl.pallas_call(
        functools.partial(chain_kernel, rows),
        in_specs=[smem, pl.BlockSpec(memory_space=pltpu.VMEM), pl.BlockSpec(memory_space=pltpu.VMEM)],
        out_specs=pl.BlockSpec(memory_space=pltpu.VMEM),
        out_shape=jax.ShapeDtypeStruct((count, poles, slim), BF16),
        name="chain",
    )(contig_lengths, pieces, mine)
    arrived = lax.all_to_all(chained, "ctx", 0, 1, tiled=False).reshape(poles, channels)

    def at(phase, j):
        return jnp.where(phase == 0, j, steps - 1)

    def per_block(shape):
        lead = (0,) * (len(shape) - 1)
        return pl.BlockSpec(shape, lambda phase, j: lead + (at(phase, j),))

    def plane_two(i):
        return pl.BlockSpec((1, rows, columns), lambda phase, j: (i, 0, at(phase, j)))

    def still(array):
        return pl.BlockSpec(array.shape, lambda phase, j: (0,) * array.ndim)

    if fused:
        out_map = lambda phase, j: (0, jnp.where(phase == 0, 0, j))
    else:
        out_map = lambda phase, j: (0, j)
    result, squares = pl.pallas_call(
        functools.partial(output_kernel, fused),
        grid=(2 if fused else 1, steps),
        in_specs=[
            smem,
            plane_two(0),
            plane_two(1),
            plane_two(2),
            per_block((3, 2, columns)),
            per_block((3, 3, columns)),
            per_block((poles, columns)),
            per_block((poles, columns)),
            per_block((1, columns)),
            pl.BlockSpec((1, columns), lambda phase, j: (0, j)),
            per_block((poles, columns)),
            still(gather),
            still(spread),
            still(near),
        ],
        out_specs=[pl.BlockSpec((rows, columns), out_map), pl.BlockSpec((rows, 128), lambda phase, j: (0, 0))],
        out_shape=[
            jax.ShapeDtypeStruct((rows, channels), BF16 if fused else F32),
            jax.ShapeDtypeStruct((rows, 128), F32),
        ],
        scratch_shapes=[
            pltpu.VMEM((2, rows, 128), F32),
            pltpu.VMEM((2 * gather.shape[0], rows), BF16),
            pltpu.VMEM((rows, 2 * spread.shape[1]), BF16),
            pltpu.VMEM(near.shape, BF16),
            pltpu.VMEM((steps, rows, columns) if fused else (1, 8, 128), F32),
        ],
        compiler_params=pltpu.CompilerParams(vmem_limit_bytes=48 << 20),
        name="output",
    )(
        contig_lengths,
        planes,
        planes,
        planes,
        edge,
        short_taps,
        decay_rate,
        residue,
        skip_gain.reshape(1, channels),
        norm_gain.reshape(1, channels),
        arrived,
        gather,
        spread,
        near,
    )
    if fused:
        return result
    mean = lax.psum(jnp.sum(squares, axis=1, keepdims=True), "chan") / D
    return (result * lax.rsqrt(mean + eps_norm) * norm_gain[None, :]).astype(BF16)


def solution(mesh):
    placed = (
        P("ctx", None, "chan"),
        P(None, None, "chan"),
        P(None, "chan"),
        P(None, "chan"),
        P("chan"),
        P("chan"),
        P(),
    )
    return jax.shard_map(
        shards, mesh=mesh, in_specs=placed, out_specs=P("ctx", "chan"), check_vma=False
    )
```

```python
import functools

import jax
import jax.numpy as jnp
import numpy as np
from jax import lax
from jax.experimental import pallas as pl
from jax.experimental.pallas import tpu as pltpu
from jax.sharding import PartitionSpec as P

D = 8192
eps_norm = 1e-05
RATE_TOP = 1.0 / 30.0 * (1.0 + 1e-6)
BLOCK = 32
WIDE = 16
NEAR = 7
TEAM = 8
CHUNK = 256
F32 = jnp.float32
BF16 = jnp.bfloat16


def nodes_of(count):
    angle = (2 * np.arange(count) + 1) * np.pi / (2 * count)
    return RATE_TOP / 2 * (1 - np.cos(angle))


def lagrange(rate, nodes):
    count = len(nodes)
    unit = nodes / RATE_TOP
    scaled = rate * F32(1.0 / RATE_TOP)
    gaps = [scaled - F32(u) for u in unit]
    ahead = [None] * count
    for i in range(1, count):
        ahead[i] = gaps[i - 1] if i == 1 else ahead[i - 1] * gaps[i - 1]
    weights = [None] * count
    after = None
    for i in reversed(range(count)):
        norm = F32(1.0 / np.prod([unit[i] - unit[j] for j in range(count) if j != i]))
        if after is None:
            weights[i] = ahead[i] * norm
            after = gaps[i]
        else:
            weights[i] = (after if i == 0 else ahead[i] * after) * norm
            after = after * gaps[i]
    return weights


def gather_matrix(rows):
    nodes = nodes_of(WIDE)
    index = np.arange(rows // BLOCK * WIDE)
    end = (index // WIDE + 1) * BLOCK - 1
    lag = end[:, None] - np.arange(rows)[None, :]
    return np.where(lag >= 0, np.exp(-nodes[index % WIDE][:, None] * np.maximum(lag, 0)), 0.0)


def spread_matrix(rows):
    nodes = nodes_of(WIDE)
    blocks = rows // BLOCK
    index = np.arange(blocks * WIDE)
    group = index // WIDE
    place = np.arange(rows)[:, None]
    end = np.where(group == blocks - 1, -1, (group + 1) * BLOCK - 1)[None, :]
    used = (group == blocks - 1)[None, :] | (place // BLOCK == group[None, :] + 1)
    lag = place - end
    return np.where(used, np.exp(-nodes[index % WIDE][None, :] * np.maximum(lag, 0)), 0.0)


def near_matrices(rows):
    lag = np.arange(rows)[:, None] - np.arange(rows)[None, :]
    same = (np.arange(rows)[:, None] // BLOCK == np.arange(rows)[None, :] // BLOCK) & (lag >= 0)
    return np.stack(
        [np.where(same, np.exp(-node * np.maximum(lag, 0)), 0.0) for node in nodes_of(NEAR)]
    )


def bounds_of(lengths_ref, anchor):
    total = -anchor
    bounds = []
    for i in range(lengths_ref.shape[0] - 1):
        total = total + lengths_ref[i]
        bounds.append(total)
    return bounds


def seg_of(place, bounds):
    return sum((place >= b).astype(jnp.int32) for b in bounds)


def halves(value):
    high = value.astype(BF16)
    return high, (value - high.astype(F32)).astype(BF16)


def product_of(left, right):
    return jnp.dot(left, right, preferred_element_type=F32)


def wide(column, columns):
    return jnp.concatenate([column] * (columns // column.shape[1]), axis=1)


def fill_keeps(keep_ref, bounds):
    rows = keep_ref.shape[1]
    place = lax.broadcasted_iota(jnp.int32, (rows, 128), 0)
    segment = seg_of(place, bounds)
    for i in range(2):
        keep_ref[i] = (seg_of(place - (i + 1), bounds) == segment).astype(F32)


def mix(block, edge, taps, keep_ref):
    rows, columns = block.shape
    now = block.astype(F32)
    edge = edge.astype(F32)
    row = lax.broadcasted_iota(jnp.int32, (rows, columns), 0)
    one = jnp.where(row == 0, edge[1:2], pltpu.roll(now, 1, 0))
    two = pltpu.roll(now, 2, 0)
    two = jnp.where(row == 0, edge[0:1], jnp.where(row == 1, edge[1:2], two))
    return (
        taps[0:1] * now
        + taps[1:2] * (one * wide(keep_ref[0], columns))
        + taps[2:3] * (two * wide(keep_ref[1], columns))
    )


def exchange_kernel(
    lengths_ref,
    planes_ref,
    taps_ref,
    rate_ref,
    gather_ref,
    arrived_ref,
    edge_ref,
    keep_ref,
    matrix_ref,
    rows_ref,
    tail_ref,
    edge_send,
    edge_land,
    local_send,
    local_land,
    total_land,
    back_send,
    back_land,
    rows_sem,
    tail_sem,
    edge_sem,
    local_sem,
    total_sem,
    back_sem,
):
    rows, channels = planes_ref.shape[1:]
    half = channels // 2
    count = lax.axis_size("ctx")
    teams = count // TEAM
    slim = channels // TEAM
    chunk = min(CHUNK, slim)
    me = lax.axis_index("ctx")
    team, rank = me // TEAM, me % TEAM

    def mate(k):
        return team * TEAM + (rank + k) % TEAM

    def peer(k):
        return (team + k) % teams * TEAM + rank

    def span(k):
        return pl.ds(pl.multiple_of((rank + k) % TEAM * slim, 128), slim)

    def load(k):
        return pltpu.make_async_copy(
            planes_ref.at[pl.ds(1, 2), :, span(k)], rows_ref.at[:, :, span(k)], rows_sem.at[k]
        )

    tail = pltpu.make_async_copy(planes_ref.at[:, pl.ds(rows - 16, 16), :], tail_ref, tail_sem)
    tail.start()
    for k in range(TEAM):
        load((k + 1) % TEAM).start()

    barrier = pltpu.get_barrier_semaphore()
    others = [mate(k) for k in range(1, TEAM)] + [peer(k) for k in range(1, teams)]
    others += [(me + 1) % count, (me + count - 1) % count]
    for other in others:
        pl.semaphore_signal(barrier, inc=1, device_id={"ctx": other}, device_id_type=pl.DeviceIdType.MESH)

    bounds = bounds_of(lengths_ref, me * rows)
    zero_bounds = bounds_of(lengths_ref, 0)
    fill_keeps(keep_ref, bounds)
    place = lax.broadcasted_iota(jnp.int32, (WIDE, rows), 1)
    same = seg_of(place, bounds) == seg_of(jnp.full((WIDE, rows), rows - 1, jnp.int32), bounds)
    high, low = halves(jnp.where(same, gather_ref[...], 0.0))
    matrix_ref[:WIDE] = high
    matrix_ref[WIDE:] = low
    tail.wait()
    ends = [tail_ref[i].astype(F32)[14:16] for i in range(3)]
    packed = [e[:, :half] for e in ends] + [e[:, half:] for e in ends] + [jnp.zeros((4, half), F32)]
    edge_send[...] = jnp.concatenate(packed, axis=0).astype(BF16)

    def remote(source, target, sems, device):
        return pltpu.make_async_remote_copy(
            src_ref=source,
            dst_ref=target,
            send_sem=sems[0],
            recv_sem=sems[1],
            device_id={"ctx": device},
            device_id_type=pl.DeviceIdType.MESH,
        )

    pl.semaphore_wait(barrier, len(others))
    edge_copy = remote(edge_send, edge_land, (edge_sem.at[0], edge_sem.at[1]), (me + 1) % count)
    edge_copy.start()
    edge_copy.wait()
    landed = jnp.where(me == 0, 0.0, edge_land[...].astype(F32))
    blank = jnp.zeros((2, half), F32)
    edge_ref[:, :half] = jnp.concatenate([landed[0:6], blank], axis=0)
    edge_ref[:, half:] = jnp.concatenate([landed[6:12], blank], axis=0)

    def local_copy(k):
        return remote(local_send.at[k], local_land.at[k], (local_sem.at[k, 0], local_sem.at[k, 1]), mate(k))

    def one_slice(k, into):
        load(k).wait()
        base = (rank + k) % TEAM * slim

        def one_chunk(i, carry):
            here = pl.ds(pl.multiple_of(base + i * chunk, 128), chunk)
            key = mix(rows_ref[0, :, here], edge_ref[2:4, here], taps_ref[:, 1, here], keep_ref)
            value = mix(rows_ref[1, :, here], edge_ref[4:6, here], taps_ref[:, 2, here], keep_ref)
            high, low = halves(key * value)
            moments = product_of(matrix_ref[...], high)
            moments = moments[:WIDE] + moments[WIDE:] + product_of(matrix_ref[:WIDE], low)
            weights = lagrange(rate_ref[:, here], nodes_of(WIDE))
            state = weights[0] * moments[0:1]
            for n in range(1, WIDE):
                state = state + weights[n] * moments[n : n + 1]
            into[k, :, pl.ds(pl.multiple_of(i * chunk, 128), chunk)] = state.astype(BF16)
            return carry

        lax.fori_loop(0, slim // chunk, one_chunk, 0)

    def send_slice(k, carry):
        one_slice(k, local_send)
        local_copy(k).start()
        return carry

    lax.fori_loop(1, TEAM, send_slice, 0)
    one_slice(0, local_land)

    mine = pl.ds(pl.multiple_of(rank * slim, 128), slim)
    rate = rate_ref[:, mine]
    fade = jnp.exp(-rate * F32(rows))
    fade_team = jnp.exp(-rate * F32(rows * TEAM))

    def whole(first, devices):
        start = first * rows
        kept = seg_of(start + devices * rows - 1, zero_bounds) == seg_of(start - 1, zero_bounds)
        return kept.astype(F32)

    for k in range(1, TEAM):
        local_copy(k).wait()
    local = [local_land[(rank + TEAM - s) % TEAM].astype(F32) for s in range(TEAM)]
    total = local[0]
    for s in range(1, TEAM):
        total = total * (fade * whole(team * TEAM + s, 1)) + local[s]
    total_land[0] = total.astype(BF16)

    def total_copy(k):
        return remote(total_land.at[0], total_land.at[k], (total_sem.at[k, 0], total_sem.at[k, 1]), peer(k))

    for k in range(1, teams):
        total_copy(k).start()
    for k in range(1, teams):
        total_copy(k).wait()
    state = jnp.zeros(rate.shape, F32)
    for g in range(teams - 1):
        after = state * (fade_team * whole(g * TEAM, TEAM)) + total_land[(team + teams - g) % teams].astype(F32)
        state = jnp.where(g < team, after, state)
    for s in range(TEAM):
        back_send[s] = state.astype(BF16)
        if s < TEAM - 1:
            state = state * (fade * whole(team * TEAM + s, 1)) + local[s]

    def back_copy(k):
        return remote(back_send.at[(rank + k) % TEAM], back_land.at[k], (back_sem.at[k, 0], back_sem.at[k, 1]), mate(k))

    for k in range(1, TEAM):
        back_copy(k).start()
    arrived_ref[:, mine] = back_send[rank]
    for k in range(1, TEAM):
        back_copy(k).wait()
    for k in range(1, TEAM):
        arrived_ref[:, span(TEAM - k)] = back_land[k]


def output_kernel(
    fused,
    lengths_ref,
    query_ref,
    key_ref,
    value_ref,
    edge_ref,
    taps_ref,
    rate_ref,
    residue_ref,
    skip_ref,
    gain_ref,
    arrived_ref,
    gather_ref,
    spread_ref,
    near_ref,
    out_ref,
    square_ref,
    keep_ref,
    gather_m,
    spread_m,
    near_m,
    held_ref,
):
    rows, columns = query_ref.shape[1:]
    phase, step = pl.program_id(0), pl.program_id(1)
    bounds = bounds_of(lengths_ref, lax.axis_index("ctx") * rows)

    @pl.when((phase == 0) & (step == 0))
    def _():
        fill_keeps(keep_ref, bounds)
        square_ref[...] = jnp.zeros_like(square_ref)
        across = lax.broadcasted_iota(jnp.int32, (rows, rows), 1)
        down = lax.broadcasted_iota(jnp.int32, (rows, rows), 0)
        count = gather_ref.shape[0]
        group = lax.broadcasted_iota(jnp.int32, (count, rows), 0) // WIDE
        same = seg_of(lax.broadcasted_iota(jnp.int32, (count, rows), 1), bounds) == seg_of(
            group * BLOCK + (BLOCK - 1), bounds
        )
        high, low = halves(jnp.where(same, gather_ref[...], 0.0))
        gather_m[:count] = high
        gather_m[count:] = low
        group = lax.broadcasted_iota(jnp.int32, (rows, count), 1) // WIDE
        end = jnp.where(group == rows // BLOCK - 1, -1, group * BLOCK + (BLOCK - 1))
        same = seg_of(lax.broadcasted_iota(jnp.int32, (rows, count), 0), bounds) == seg_of(end, bounds)
        high, low = halves(jnp.where(same, spread_ref[...], 0.0))
        spread_m[:, :count] = high
        spread_m[:, count:] = low
        same = seg_of(down, bounds) == seg_of(across, bounds)
        for i in range(NEAR):
            near_m[i] = jnp.where(same, near_ref[i].astype(F32), 0.0).astype(BF16)

    @pl.when(phase == 0)
    def _():
        chunk = min(CHUNK, columns)

        def one_chunk(index, carry):
            here = pl.ds(pl.multiple_of(index * chunk, 128), chunk)
            product = mix(key_ref[0, :, here], edge_ref[2:4, here], taps_ref[:, 1, here], keep_ref) * mix(
                value_ref[0, :, here], edge_ref[4:6, here], taps_ref[:, 2, here], keep_ref
            )
            rate = rate_ref[:, here]
            scale = residue_ref[:, here] * jnp.sqrt(1.0 - jnp.exp(-2.0 * rate))
            brought = scale * arrived_ref[:, here].astype(F32)
            weights = lagrange(rate, nodes_of(WIDE))
            share = jnp.concatenate([jnp.sum(w * scale, axis=0, keepdims=True) for w in weights], axis=0)
            entry = jnp.concatenate([jnp.sum(w * brought, axis=0, keepdims=True) for w in weights], axis=0)
            near = [jnp.sum(w * scale, axis=0, keepdims=True) for w in lagrange(rate, nodes_of(NEAR))]
            high, low = halves(product)
            total = skip_ref[:, here] * product
            for i in range(NEAR):
                total = total + near[i] * product_of(near_m[i], high)
            count = gather_ref.shape[0]
            moments = product_of(gather_m[...], high)
            moments = moments[:count] + moments[count:] + product_of(gather_m[:count], low)
            last = count - WIDE
            moments = (moments[:last].reshape(-1, WIDE, chunk) * share[None]).reshape(last, chunk)
            high, low = halves(jnp.concatenate([moments, entry], axis=0))
            total = total + product_of(spread_m[...], jnp.concatenate([high, high], axis=0))
            total = total + product_of(spread_m[:, :count], low)
            response = mix(query_ref[0, :, here], edge_ref[0:2, here], taps_ref[:, 0, here], keep_ref) * total
            squares = response * response
            part = squares[:, :128]
            for i in range(1, chunk // 128):
                part = part + squares[:, i * 128 : (i + 1) * 128]
            square_ref[...] += part
            if fused:
                held_ref[step, :, here] = response
            else:
                out_ref[:, here] = response
            return carry

        lax.fori_loop(0, columns // chunk, one_chunk, 0)

    if fused:

        @pl.when((phase == 1) & (step == 0))
        def _():
            mean = jnp.sum(square_ref[...], axis=1, keepdims=True) / D
            square_ref[...] = jnp.broadcast_to(lax.rsqrt(mean + eps_norm), square_ref.shape)

        @pl.when(phase == 1)
        def _():
            out_ref[...] = (held_ref[step] * wide(square_ref[...], columns) * gain_ref[...]).astype(BF16)


def shards(features, short_taps, decay_rate, residue, skip_gain, norm_gain, contig_lengths):
    rows, _, channels = features.shape
    count = lax.axis_size("ctx")
    fused = lax.axis_size("chan") == 1
    poles = decay_rate.shape[0]
    planes = jnp.transpose(features, (1, 0, 2))
    columns = min(1024, channels)
    steps = channels // columns
    gather = jnp.asarray(gather_matrix(rows), F32)
    spread = jnp.asarray(spread_matrix(rows), F32)
    near = jnp.asarray(near_matrices(rows), BF16)
    smem = pl.BlockSpec(memory_space=pltpu.SMEM)

    vmem = pl.BlockSpec(memory_space=pltpu.VMEM)
    slim = channels // TEAM
    teams = count // TEAM
    arrived, edge = pl.pallas_call(
        exchange_kernel,
        in_specs=[smem, pl.BlockSpec(memory_space=pl.ANY), vmem, vmem, vmem],
        out_specs=[vmem, vmem],
        out_shape=[
            jax.ShapeDtypeStruct((poles, channels), BF16),
            jax.ShapeDtypeStruct((8, channels), F32),
        ],
        scratch_shapes=[
            pltpu.VMEM((2, rows, 128), F32),
            pltpu.VMEM((2 * WIDE, rows), BF16),
            pltpu.VMEM((2, rows, channels), BF16),
            pltpu.VMEM((3, 16, channels), BF16),
            pltpu.VMEM((16, channels // 2), BF16),
            pltpu.VMEM((16, channels // 2), BF16),
            pltpu.VMEM((TEAM, poles, slim), BF16),
            pltpu.VMEM((TEAM, poles, slim), BF16),
            pltpu.VMEM((teams, poles, slim), BF16),
            pltpu.VMEM((TEAM, poles, slim), BF16),
            pltpu.VMEM((TEAM, poles, slim), BF16),
            pltpu.SemaphoreType.DMA((TEAM,)),
            pltpu.SemaphoreType.DMA,
            pltpu.SemaphoreType.DMA((2,)),
            pltpu.SemaphoreType.DMA((TEAM, 2)),
            pltpu.SemaphoreType.DMA((teams, 2)),
            pltpu.SemaphoreType.DMA((TEAM, 2)),
        ],
        compiler_params=pltpu.CompilerParams(
            collective_id=0, has_side_effects=True, vmem_limit_bytes=60 << 20
        ),
        name="exchange",
    )(contig_lengths, planes, short_taps, decay_rate, jnp.asarray(gather_matrix(rows)[-WIDE:], F32))

    def at(phase, j):
        return jnp.where(phase == 0, j, steps - 1)

    def per_block(shape):
        lead = (0,) * (len(shape) - 1)
        return pl.BlockSpec(shape, lambda phase, j: lead + (at(phase, j),))

    def plane_two(i):
        return pl.BlockSpec((1, rows, columns), lambda phase, j: (i, 0, at(phase, j)))

    def still(array):
        return pl.BlockSpec(array.shape, lambda phase, j: (0,) * array.ndim)

    if fused:
        out_map = lambda phase, j: (0, jnp.where(phase == 0, 0, j))
    else:
        out_map = lambda phase, j: (0, j)
    result, squares = pl.pallas_call(
        functools.partial(output_kernel, fused),
        grid=(2 if fused else 1, steps),
        in_specs=[
            smem,
            plane_two(0),
            plane_two(1),
            plane_two(2),
            per_block((8, columns)),
            per_block((3, 3, columns)),
            per_block((poles, columns)),
            per_block((poles, columns)),
            per_block((1, columns)),
            pl.BlockSpec((1, columns), lambda phase, j: (0, j)),
            per_block((poles, columns)),
            still(gather),
            still(spread),
            still(near),
        ],
        out_specs=[pl.BlockSpec((rows, columns), out_map), pl.BlockSpec((rows, 128), lambda phase, j: (0, 0))],
        out_shape=[
            jax.ShapeDtypeStruct((rows, channels), BF16 if fused else F32),
            jax.ShapeDtypeStruct((rows, 128), F32),
        ],
        scratch_shapes=[
            pltpu.VMEM((2, rows, 128), F32),
            pltpu.VMEM((2 * gather.shape[0], rows), BF16),
            pltpu.VMEM((rows, 2 * spread.shape[1]), BF16),
            pltpu.VMEM(near.shape, BF16),
            pltpu.VMEM((steps, rows, columns) if fused else (1, 8, 128), F32),
        ],
        compiler_params=pltpu.CompilerParams(vmem_limit_bytes=60 << 20),
        name="output",
    )(
        contig_lengths,
        planes,
        planes,
        planes,
        edge,
        short_taps,
        decay_rate,
        residue,
        skip_gain.reshape(1, channels),
        norm_gain.reshape(1, channels),
        arrived,
        gather,
        spread,
        near,
    )
    if fused:
        return result
    mean = lax.psum(jnp.sum(squares, axis=1, keepdims=True), "chan") / D
    return (result * lax.rsqrt(mean + eps_norm) * norm_gain[None, :]).astype(BF16)


def solution(mesh):
    placed = (
        P("ctx", None, "chan"),
        P(None, None, "chan"),
        P(None, "chan"),
        P(None, "chan"),
        P("chan"),
        P("chan"),
        P(),
    )
    return jax.shard_map(
        shards, mesh=mesh, in_specs=placed, out_specs=P("ctx", "chan"), check_vma=False
    )
```

```python
import functools

import jax
import jax.numpy as jnp
import numpy as np
from jax import lax
from jax.experimental import pallas as pl
from jax.experimental.pallas import tpu as pltpu
from jax.sharding import PartitionSpec as P

D = 8192
eps_norm = 1e-05
RATE_TOP = 1.0 / 30.0 * (1.0 + 1e-6)
BLOCK = 32
WIDE = 16
NEAR = 7
TEAM = 8
CHUNK = 256
F32 = jnp.float32
BF16 = jnp.bfloat16


def nodes_of(count):
    angle = (2 * np.arange(count) + 1) * np.pi / (2 * count)
    return RATE_TOP / 2 * (1 - np.cos(angle))


def lagrange(rate, nodes):
    count = len(nodes)
    unit = nodes / RATE_TOP
    scaled = rate * F32(1.0 / RATE_TOP)
    gaps = [scaled - F32(u) for u in unit]
    ahead = [None] * count
    for i in range(1, count):
        ahead[i] = gaps[i - 1] if i == 1 else ahead[i - 1] * gaps[i - 1]
    weights = [None] * count
    after = None
    for i in reversed(range(count)):
        norm = F32(1.0 / np.prod([unit[i] - unit[j] for j in range(count) if j != i]))
        if after is None:
            weights[i] = ahead[i] * norm
            after = gaps[i]
        else:
            weights[i] = (after if i == 0 else ahead[i] * after) * norm
            after = after * gaps[i]
    return weights


def gather_matrix(rows):
    nodes = nodes_of(WIDE)
    index = np.arange(rows // BLOCK * WIDE)
    end = (index // WIDE + 1) * BLOCK - 1
    lag = end[:, None] - np.arange(rows)[None, :]
    return np.where(lag >= 0, np.exp(-nodes[index % WIDE][:, None] * np.maximum(lag, 0)), 0.0)


def spread_matrix(rows):
    nodes = nodes_of(WIDE)
    index = np.arange(rows // BLOCK * WIDE)
    group = index // WIDE
    place = np.arange(rows)[:, None]
    lag = place - ((group + 1) * BLOCK - 1)[None, :]
    used = place // BLOCK == group[None, :] + 1
    return np.where(used, np.exp(-nodes[index % WIDE][None, :] * np.maximum(lag, 0)), 0.0)


def entry_matrix(rows):
    return np.exp(-nodes_of(WIDE)[None, :] * (np.arange(rows)[:, None] + 1.0))


def near_matrices(rows):
    lag = np.arange(rows)[:, None] - np.arange(rows)[None, :]
    same = (np.arange(rows)[:, None] // BLOCK == np.arange(rows)[None, :] // BLOCK) & (lag >= 0)
    return np.stack(
        [np.where(same, np.exp(-node * np.maximum(lag, 0)), 0.0) for node in nodes_of(NEAR)]
    )


def bounds_of(lengths_ref, anchor):
    total = -anchor
    bounds = []
    for i in range(lengths_ref.shape[0] - 1):
        total = total + lengths_ref[i]
        bounds.append(total)
    return bounds


def seg_of(place, bounds):
    return sum((place >= b).astype(jnp.int32) for b in bounds)


def halves(value):
    high = value.astype(BF16)
    return high, (value - high.astype(F32)).astype(BF16)


def product_of(left, right):
    return jnp.dot(left, right, preferred_element_type=F32)


def wide(column, columns):
    return jnp.concatenate([column] * (columns // column.shape[1]), axis=1)


def fill_keeps(keep_ref, edge_keep_ref, bounds):
    rows = keep_ref.shape[1]
    place = lax.broadcasted_iota(jnp.int32, (rows, 128), 0)
    segment = seg_of(place, bounds)
    for i in range(2):
        keep = (seg_of(place - (i + 1), bounds) == segment).astype(F32)
        keep_ref[i] = jnp.where(place > i, keep, 0.0)
        edge_keep_ref[i] = jnp.where(place > i, 0.0, keep)[:8]


def mix(block, edge, taps, keep_ref, edge_keep_ref):
    columns = block.shape[1]
    now = block.astype(F32)
    mixed = (
        taps[0:1] * now
        + taps[1:2] * (pltpu.roll(now, 1, 0) * wide(keep_ref[0], columns))
        + taps[2:3] * (pltpu.roll(now, 2, 0) * wide(keep_ref[1], columns))
    )
    row = lax.broadcasted_iota(jnp.int32, (8, columns), 0)
    one = jnp.where(row == 0, edge[1:2], 0.0) * wide(edge_keep_ref[0], columns)
    two = jnp.where(row == 0, edge[0:1], jnp.where(row == 1, edge[1:2], 0.0)) * wide(edge_keep_ref[1], columns)
    return jnp.concatenate([mixed[:8] + (taps[1:2] * one + taps[2:3] * two), mixed[8:]], axis=0)


def exchange_kernel(
    lengths_ref,
    planes_ref,
    taps_ref,
    rate_ref,
    residue_ref,
    skip_ref,
    gather_ref,
    spread_ref,
    near_ref,
    entry_ref,
    edge_ref,
    total_ref,
    keep_ref,
    edge_keep_ref,
    matrix_ref,
    gather_m,
    spread_m,
    near_m,
    drive_ref,
    weight_ref,
    arrived_ref,
    rows_ref,
    tail_ref,
    edge_send,
    edge_land,
    local_send,
    local_land,
    total_land,
    back_send,
    back_land,
    rows_sem,
    tail_sem,
    edge_sem,
    local_sem,
    total_sem,
    back_sem,
    out_sem,
):
    rows, channels = planes_ref.shape[1:]
    half = channels // 2
    count = lax.axis_size("ctx")
    teams = count // TEAM
    slim = channels // TEAM
    chunk = min(CHUNK, slim)
    me = lax.axis_index("ctx")
    team, rank = me // TEAM, me % TEAM

    def mate(k):
        return team * TEAM + (rank + k) % TEAM

    def peer(k):
        return (team + k) % teams * TEAM + rank

    def span(k):
        return pl.ds(pl.multiple_of((rank + k) % TEAM * slim, 128), slim)

    def load(k):
        return pltpu.make_async_copy(
            planes_ref.at[pl.ds(1, 2), :, span(k)], rows_ref.at[:, :, span(k)], rows_sem.at[k]
        )

    tail = pltpu.make_async_copy(planes_ref.at[:, pl.ds(rows - 16, 16), :], tail_ref, tail_sem)
    tail.start()
    for k in range(TEAM):
        load((k + 1) % TEAM).start()

    barrier = pltpu.get_barrier_semaphore()
    others = [mate(k) for k in range(1, TEAM)] + [peer(k) for k in range(1, teams)]
    others += [(me + 1) % count, (me + count - 1) % count]
    for other in others:
        pl.semaphore_signal(barrier, inc=1, device_id={"ctx": other}, device_id_type=pl.DeviceIdType.MESH)

    bounds = bounds_of(lengths_ref, me * rows)
    zero_bounds = bounds_of(lengths_ref, 0)
    fill_keeps(keep_ref, edge_keep_ref, bounds)
    groups = gather_ref.shape[0]
    place = lax.broadcasted_iota(jnp.int32, (groups, rows), 1)
    end = lax.broadcasted_iota(jnp.int32, (groups, rows), 0) // WIDE * BLOCK + (BLOCK - 1)
    high, low = halves(jnp.where(seg_of(place, bounds) == seg_of(end, bounds), gather_ref[...], 0.0))
    gather_m[:groups] = high
    gather_m[groups:] = low
    matrix_ref[:WIDE] = high[groups - WIDE :]
    matrix_ref[WIDE:] = low[groups - WIDE :]
    place = lax.broadcasted_iota(jnp.int32, (rows, groups), 0)
    end = lax.broadcasted_iota(jnp.int32, (rows, groups), 1) // WIDE * BLOCK + (BLOCK - 1)
    high, low = halves(jnp.where(seg_of(place, bounds) == seg_of(end, bounds), spread_ref[...], 0.0))
    spread_m[:, :groups] = high
    spread_m[:, groups:] = low
    across = lax.broadcasted_iota(jnp.int32, (rows, rows), 1)
    down = lax.broadcasted_iota(jnp.int32, (rows, rows), 0)
    same = seg_of(down, bounds) == seg_of(across, bounds)
    for i in range(NEAR):
        near_m[i] = jnp.where(same, near_ref[i].astype(F32), 0.0).astype(BF16)
    tail.wait()
    ends = [tail_ref[i].astype(F32)[14:16] for i in range(3)]
    packed = [e[:, :half] for e in ends] + [e[:, half:] for e in ends] + [jnp.zeros((4, half), F32)]
    edge_send[...] = jnp.concatenate(packed, axis=0).astype(BF16)

    def remote(source, target, sems, device):
        return pltpu.make_async_remote_copy(
            src_ref=source,
            dst_ref=target,
            send_sem=sems[0],
            recv_sem=sems[1],
            device_id={"ctx": device},
            device_id_type=pl.DeviceIdType.MESH,
        )

    pl.semaphore_wait(barrier, len(others))
    edge_copy = remote(edge_send, edge_land, (edge_sem.at[0], edge_sem.at[1]), (me + 1) % count)
    edge_copy.start()
    edge_copy.wait()
    landed = jnp.where(me == 0, 0.0, edge_land[...].astype(F32))
    blank = jnp.zeros((2, half), F32)
    edge_ref[:, :half] = jnp.concatenate([landed[0:6], blank], axis=0)
    edge_ref[:, half:] = jnp.concatenate([landed[6:12], blank], axis=0)

    def local_copy(k):
        return remote(local_send.at[k], local_land.at[k], (local_sem.at[k, 0], local_sem.at[k, 1]), mate(k))

    def one_slice(k, into):
        load(k).wait()
        base = (rank + k) % TEAM * slim

        def one_chunk(i, carry):
            here = pl.ds(pl.multiple_of(base + i * chunk, 128), chunk)
            key = mix(rows_ref[0, :, here], edge_ref[2:4, here], taps_ref[:, 1, here], keep_ref, edge_keep_ref)
            value = mix(rows_ref[1, :, here], edge_ref[4:6, here], taps_ref[:, 2, here], keep_ref, edge_keep_ref)
            drive = key * value
            drive_ref[:, here] = drive
            high, low = halves(drive)
            moments = product_of(matrix_ref[...], high)
            moments = moments[:WIDE] + moments[WIDE:] + product_of(matrix_ref[:WIDE], low)
            rate = rate_ref[:, here]
            scale = residue_ref[:, here] * jnp.sqrt(1.0 - jnp.exp(-2.0 * rate))
            weights = lagrange(rate, nodes_of(WIDE))
            for n in range(WIDE):
                weight_ref[n, :, here] = weights[n] * scale
            state = weights[0] * moments[0:1]
            for n in range(1, WIDE):
                state = state + weights[n] * moments[n : n + 1]
            into[k, :, pl.ds(pl.multiple_of(i * chunk, 128), chunk)] = state.astype(BF16)
            return carry

        lax.fori_loop(0, slim // chunk, one_chunk, 0)

    def send_slice(k, carry):
        one_slice(k, local_send)
        local_copy(k).start()
        return carry

    lax.fori_loop(1, TEAM, send_slice, 0)
    one_slice(0, local_land)

    def out_copy(k):
        return pltpu.make_async_copy(drive_ref.at[:, span(k)], total_ref.at[:, span(k)], out_sem.at[k])

    def filter_slice(k, carry):
        base = (rank + k) % TEAM * slim

        def one_chunk(i, carry):
            here = pl.ds(pl.multiple_of(base + i * chunk, 128), chunk)
            rate = rate_ref[:, here]
            scale = residue_ref[:, here] * jnp.sqrt(1.0 - jnp.exp(-2.0 * rate))
            close = [jnp.sum(w * scale, axis=0, keepdims=True) for w in lagrange(rate, nodes_of(NEAR))]
            share = jnp.concatenate(
                [jnp.sum(weight_ref[n, :, here], axis=0, keepdims=True) for n in range(WIDE)], axis=0
            )
            drive = drive_ref[:, here]
            high, low = halves(drive)
            total = skip_ref[:, here] * drive
            for n in range(NEAR):
                total = total + close[n] * product_of(near_m[n], high)
            moments = product_of(gather_m[...], high)
            moments = moments[:groups] + moments[groups:] + product_of(gather_m[:groups], low)
            moments = (moments.reshape(-1, WIDE, chunk) * share[None]).reshape(groups, chunk)
            high, low = halves(moments)
            total = total + product_of(spread_m[...], jnp.concatenate([high, high], axis=0))
            total = total + product_of(spread_m[:, :groups], low)
            drive_ref[:, here] = total
            return carry

        lax.fori_loop(0, slim // chunk, one_chunk, 0)
        out_copy(k).start()
        return carry

    lax.fori_loop(0, 2, filter_slice, 0)

    mine = pl.ds(pl.multiple_of(rank * slim, 128), slim)
    rate = rate_ref[:, mine]
    fade = jnp.exp(-rate * F32(rows))
    fade_team = jnp.exp(-rate * F32(rows * TEAM))

    def whole(first, devices):
        start = first * rows
        kept = seg_of(start + devices * rows - 1, zero_bounds) == seg_of(start - 1, zero_bounds)
        return kept.astype(F32)

    for k in range(1, TEAM):
        local_copy(k).wait()
    local = [local_land[(rank + TEAM - s) % TEAM].astype(F32) for s in range(TEAM)]
    total = local[0]
    for s in range(1, TEAM):
        total = total * (fade * whole(team * TEAM + s, 1)) + local[s]
    total_land[0] = total.astype(BF16)

    def total_copy(k):
        return remote(total_land.at[0], total_land.at[k], (total_sem.at[k, 0], total_sem.at[k, 1]), peer(k))

    for k in range(1, teams):
        total_copy(k).start()
    lax.fori_loop(2, 5, filter_slice, 0)
    for k in range(1, teams):
        total_copy(k).wait()
    state = jnp.zeros(rate.shape, F32)
    for g in range(teams - 1):
        after = state * (fade_team * whole(g * TEAM, TEAM)) + total_land[(team + teams - g) % teams].astype(F32)
        state = jnp.where(g < team, after, state)
    for s in range(TEAM):
        back_send[s] = state.astype(BF16)
        if s < TEAM - 1:
            state = state * (fade * whole(team * TEAM + s, 1)) + local[s]

    def back_copy(k):
        return remote(back_send.at[(rank + k) % TEAM], back_land.at[k], (back_sem.at[k, 0], back_sem.at[k, 1]), mate(k))

    for k in range(1, TEAM):
        back_copy(k).start()
    arrived_ref[:, mine] = back_send[rank]
    lax.fori_loop(5, TEAM, filter_slice, 0)
    for k in range(1, TEAM):
        back_copy(k).wait()
    for k in range(1, TEAM):
        arrived_ref[:, span(TEAM - k)] = back_land[k]

    def entry_chunk(i, carry):
        here = pl.ds(pl.multiple_of(i * chunk, 128), chunk)
        arrived = arrived_ref[:, here].astype(F32)
        entry_ref[:, here] = jnp.concatenate(
            [jnp.sum(weight_ref[n, :, here] * arrived, axis=0, keepdims=True) for n in range(WIDE)], axis=0
        )
        return carry

    lax.fori_loop(0, channels // chunk, entry_chunk, 0)
    for k in range(TEAM):
        out_copy(k).wait()


def output_kernel(
    fused,
    lengths_ref,
    query_ref,
    total_ref,
    edge_ref,
    taps_ref,
    gain_ref,
    entry_ref,
    arrive_ref,
    out_ref,
    square_ref,
    keep_ref,
    edge_keep_ref,
    arrive_m,
    held_ref,
):
    rows, columns = query_ref.shape[1:]
    phase, step = pl.program_id(0), pl.program_id(1)

    @pl.when((phase == 0) & (step == 0))
    def _():
        bounds = bounds_of(lengths_ref, lax.axis_index("ctx") * rows)
        fill_keeps(keep_ref, edge_keep_ref, bounds)
        square_ref[...] = jnp.zeros_like(square_ref)
        place = lax.broadcasted_iota(jnp.int32, (rows, WIDE), 0)
        same = seg_of(place, bounds) == seg_of(jnp.full((rows, WIDE), -1, jnp.int32), bounds)
        high, low = halves(jnp.where(same, arrive_ref[...], 0.0))
        arrive_m[...] = jnp.concatenate([high, low, high], axis=1)

    @pl.when(phase == 0)
    def _():
        chunk = min(CHUNK, columns)

        def one_chunk(index, carry):
            here = pl.ds(pl.multiple_of(index * chunk, 128), chunk)
            high, low = halves(entry_ref[:, here])
            total = total_ref[:, here] + product_of(arrive_m[...], jnp.concatenate([high, high, low], axis=0))
            query = mix(query_ref[0, :, here], edge_ref[0:2, here], taps_ref[:, 0, here], keep_ref, edge_keep_ref)
            response = query * total
            squares = response * response
            part = squares[:, :128]
            for i in range(1, chunk // 128):
                part = part + squares[:, i * 128 : (i + 1) * 128]
            square_ref[...] += part
            if fused:
                held_ref[step, :, here] = response
            else:
                out_ref[:, here] = response
            return carry

        lax.fori_loop(0, columns // chunk, one_chunk, 0)

    if fused:

        @pl.when((phase == 1) & (step == 0))
        def _():
            mean = jnp.sum(square_ref[...], axis=1, keepdims=True) / D
            square_ref[...] = jnp.broadcast_to(lax.rsqrt(mean + eps_norm), square_ref.shape)

        @pl.when(phase == 1)
        def _():
            out_ref[...] = (held_ref[step] * wide(square_ref[...], columns) * gain_ref[...]).astype(BF16)


def shards(features, short_taps, decay_rate, residue, skip_gain, norm_gain, contig_lengths):
    rows, _, channels = features.shape
    count = lax.axis_size("ctx")
    fused = lax.axis_size("chan") == 1
    poles = decay_rate.shape[0]
    planes = jnp.transpose(features, (1, 0, 2))
    columns = min(1024, channels)
    steps = channels // columns
    gather = jnp.asarray(gather_matrix(rows), F32)
    spread = jnp.asarray(spread_matrix(rows), F32)
    near = jnp.asarray(near_matrices(rows), BF16)
    arrive = jnp.asarray(entry_matrix(rows), F32)
    smem = pl.BlockSpec(memory_space=pltpu.SMEM)

    vmem = pl.BlockSpec(memory_space=pltpu.VMEM)
    slim = channels // TEAM
    teams = count // TEAM
    groups = rows // BLOCK * WIDE
    entry, edge, total = pl.pallas_call(
        exchange_kernel,
        in_specs=[smem, pl.BlockSpec(memory_space=pl.ANY)] + [vmem] * 7,
        out_specs=[vmem, vmem, pl.BlockSpec(memory_space=pl.ANY)],
        out_shape=[
            jax.ShapeDtypeStruct((WIDE, channels), F32),
            jax.ShapeDtypeStruct((8, channels), F32),
            jax.ShapeDtypeStruct((rows, channels), F32),
        ],
        scratch_shapes=[
            pltpu.VMEM((2, rows, 128), F32),
            pltpu.VMEM((2, 8, 128), F32),
            pltpu.VMEM((2 * WIDE, rows), BF16),
            pltpu.VMEM((2 * groups, rows), BF16),
            pltpu.VMEM((rows, 2 * groups), BF16),
            pltpu.VMEM((NEAR, rows, rows), BF16),
            pltpu.VMEM((rows, channels), F32),
            pltpu.VMEM((WIDE, poles, channels), F32),
            pltpu.VMEM((poles, channels), BF16),
            pltpu.VMEM((2, rows, channels), BF16),
            pltpu.VMEM((3, 16, channels), BF16),
            pltpu.VMEM((16, channels // 2), BF16),
            pltpu.VMEM((16, channels // 2), BF16),
            pltpu.VMEM((TEAM, poles, slim), BF16),
            pltpu.VMEM((TEAM, poles, slim), BF16),
            pltpu.VMEM((teams, poles, slim), BF16),
            pltpu.VMEM((TEAM, poles, slim), BF16),
            pltpu.VMEM((TEAM, poles, slim), BF16),
            pltpu.SemaphoreType.DMA((TEAM,)),
            pltpu.SemaphoreType.DMA,
            pltpu.SemaphoreType.DMA((2,)),
            pltpu.SemaphoreType.DMA((TEAM, 2)),
            pltpu.SemaphoreType.DMA((teams, 2)),
            pltpu.SemaphoreType.DMA((TEAM, 2)),
            pltpu.SemaphoreType.DMA((TEAM,)),
        ],
        compiler_params=pltpu.CompilerParams(
            collective_id=0, has_side_effects=True, vmem_limit_bytes=60 << 20
        ),
        name="exchange",
    )(
        contig_lengths,
        planes,
        short_taps,
        decay_rate,
        residue,
        skip_gain.reshape(1, channels),
        gather,
        spread,
        near,
    )

    def at(phase, j):
        return jnp.where(phase == 0, j, steps - 1)

    def per_block(shape):
        lead = (0,) * (len(shape) - 1)
        return pl.BlockSpec(shape, lambda phase, j: lead + (at(phase, j),))

    def plane_two(i):
        return pl.BlockSpec((1, rows, columns), lambda phase, j: (i, 0, at(phase, j)))

    def still(array):
        return pl.BlockSpec(array.shape, lambda phase, j: (0,) * array.ndim)

    if fused:
        out_map = lambda phase, j: (0, jnp.where(phase == 0, 0, j))
    else:
        out_map = lambda phase, j: (0, j)
    result, squares = pl.pallas_call(
        functools.partial(output_kernel, fused),
        grid=(2 if fused else 1, steps),
        in_specs=[
            smem,
            plane_two(0),
            per_block((rows, columns)),
            per_block((8, columns)),
            per_block((3, 3, columns)),
            pl.BlockSpec((1, columns), lambda phase, j: (0, j)),
            per_block((WIDE, columns)),
            still(arrive),
        ],
        out_specs=[pl.BlockSpec((rows, columns), out_map), pl.BlockSpec((rows, 128), lambda phase, j: (0, 0))],
        out_shape=[
            jax.ShapeDtypeStruct((rows, channels), BF16 if fused else F32),
            jax.ShapeDtypeStruct((rows, 128), F32),
        ],
        scratch_shapes=[
            pltpu.VMEM((2, rows, 128), F32),
            pltpu.VMEM((2, 8, 128), F32),
            pltpu.VMEM((rows, 3 * WIDE), BF16),
            pltpu.VMEM((steps, rows, columns) if fused else (1, 8, 128), F32),
        ],
        compiler_params=pltpu.CompilerParams(vmem_limit_bytes=60 << 20),
        name="output",
    )(contig_lengths, planes, total, edge, short_taps, norm_gain.reshape(1, channels), entry, arrive)
    if fused:
        return result
    mean = lax.psum(jnp.sum(squares, axis=1, keepdims=True), "chan") / D
    return (result * lax.rsqrt(mean + eps_norm) * norm_gain[None, :]).astype(BF16)


def solution(mesh):
    placed = (
        P("ctx", None, "chan"),
        P(None, None, "chan"),
        P(None, "chan"),
        P(None, "chan"),
        P("chan"),
        P("chan"),
        P(),
    )
    return jax.shard_map(
        shards, mesh=mesh, in_specs=placed, out_specs=P("ctx", "chan"), check_vma=False
    )
```

```python
import functools

import jax
import jax.numpy as jnp
import ml_dtypes
import numpy as np
from jax import lax
from jax.experimental import pallas as pl
from jax.experimental.pallas import tpu as pltpu
from jax.sharding import PartitionSpec as P

D = 8192
eps_norm = 1e-05
RATE_TOP = 1.0 / 30.0 * (1.0 + 1e-6)
BLOCK = 32
WIDE = 16
NEAR = 6
MIDDLE = (BLOCK - 1) / 2
TEAM = 8
LEAD = 16
CHUNK = 256
F32 = jnp.float32
BF16 = jnp.bfloat16


def nodes_of(count):
    angle = (2 * np.arange(count) + 1) * np.pi / (2 * count)
    return RATE_TOP / 2 * (1 - np.cos(angle))


def lagrange(rate, nodes):
    count = len(nodes)
    unit = nodes / RATE_TOP
    scaled = rate * F32(1.0 / RATE_TOP)
    gaps = [scaled - F32(u) for u in unit]
    ahead = [None] * count
    for i in range(1, count):
        ahead[i] = gaps[i - 1] if i == 1 else ahead[i - 1] * gaps[i - 1]
    weights = [None] * count
    after = None
    for i in reversed(range(count)):
        norm = F32(1.0 / np.prod([unit[i] - unit[j] for j in range(count) if j != i]))
        if after is None:
            weights[i] = ahead[i] * norm
            after = gaps[i]
        else:
            weights[i] = (after if i == 0 else ahead[i] * after) * norm
            after = after * gaps[i]
    return weights


def split(matrix):
    high = matrix.astype(ml_dtypes.bfloat16)
    return high, (matrix - high.astype(np.float64)).astype(ml_dtypes.bfloat16)


def gather_matrix(rows):
    nodes = nodes_of(WIDE)
    index = np.arange(rows // BLOCK * WIDE)
    end = (index // WIDE + 1) * BLOCK - 1
    lag = end[:, None] - np.arange(rows)[None, :]
    matrix = np.where(lag >= 0, np.exp(-nodes[index % WIDE][:, None] * np.maximum(lag, 0)), 0.0)
    return np.concatenate(split(matrix), axis=0)


def block_matrix(rows):
    place = np.arange(rows)[:, None] % BLOCK
    lag = place - np.arange(BLOCK)[None, :]
    near = [np.where(lag >= 0, np.exp(-node * (lag - MIDDLE)), 0.0) for node in nodes_of(NEAR)]
    high, low = split(np.exp(-nodes_of(WIDE)[None, :] * (place + 1.0)))
    return np.concatenate([split(n)[0] for n in near] + [high, low, high], axis=1)


def entry_matrix(rows):
    return np.exp(-nodes_of(WIDE)[None, :] * (np.arange(rows)[:, None] + 1.0))


def near_matrices(rows):
    lag = np.arange(rows)[:, None] - np.arange(rows)[None, :]
    same = (np.arange(rows)[:, None] // BLOCK == np.arange(rows)[None, :] // BLOCK) & (lag >= 0)
    return np.stack(
        [np.where(same, np.exp(-node * np.maximum(lag, 0)), 0.0) for node in nodes_of(NEAR)]
    )


def bounds_of(lengths_ref, anchor):
    total = -anchor
    bounds = []
    for i in range(lengths_ref.shape[0] - 1):
        total = total + lengths_ref[i]
        bounds.append(total)
    return bounds


def seg_of(place, bounds):
    return sum((place >= b).astype(jnp.int32) for b in bounds)


def halves(value):
    high = value.astype(BF16)
    return high, (value - high.astype(F32)).astype(BF16)


def product_of(left, right):
    return jnp.dot(left, right, preferred_element_type=F32)


def wide(column, columns):
    return jnp.concatenate([column] * (columns // column.shape[1]), axis=1)


def shift_shape(rows):
    return (2 * rows, BLOCK + LEAD)


def fill_shifts(shift_ref, bounds):
    down = lax.broadcasted_iota(jnp.int32, shift_ref.shape, 0)
    column = lax.broadcasted_iota(jnp.int32, shift_ref.shape, 1)
    by = 1 + down % (2 * BLOCK) // BLOCK
    place = down // (2 * BLOCK) * BLOCK + down % BLOCK
    same = seg_of(place, bounds) == seg_of(place - by, bounds)
    used = same & (column == LEAD + down % BLOCK - by)
    shift_ref[...] = jnp.where(used, 1.0, 0.0).astype(BF16)


def mix(block, taps, shifts):
    moved = product_of(shifts, block)
    now = block[LEAD:].astype(F32)
    return taps[0:1] * now + taps[1:2] * moved[:BLOCK] + taps[2:3] * moved[BLOCK:]


def exchange_kernel(
    lengths_ref,
    planes_ref,
    taps_ref,
    rate_ref,
    residue_ref,
    skip_ref,
    gather_ref,
    block_ref,
    entry_ref,
    edge_ref,
    total_ref,
    shift_ref,
    matrix_ref,
    gather_m,
    block_m,
    drive_ref,
    weight_ref,
    arrived_ref,
    rows_ref,
    tail_ref,
    edge_send,
    edge_land,
    local_send,
    local_land,
    total_land,
    back_send,
    back_land,
    rows_sem,
    tail_sem,
    edge_sem,
    local_sem,
    total_sem,
    back_sem,
    out_sem,
):
    rows, channels = planes_ref.shape[1:]
    half = channels // 2
    count = lax.axis_size("ctx")
    teams = count // TEAM
    slim = channels // TEAM
    chunk = min(CHUNK, slim)
    me = lax.axis_index("ctx")
    team, rank = me // TEAM, me % TEAM

    def mate(k):
        return team * TEAM + (rank + k) % TEAM

    def peer(k):
        return (team + k) % teams * TEAM + rank

    def span(k):
        return pl.ds(pl.multiple_of((rank + k) % TEAM * slim, 128), slim)

    def load(k):
        return pltpu.make_async_copy(
            planes_ref.at[pl.ds(1, 2), :, span(k)], rows_ref.at[:, pl.ds(LEAD, rows), span(k)], rows_sem.at[k]
        )

    tail = pltpu.make_async_copy(planes_ref.at[:, pl.ds(rows - 16, 16), :], tail_ref, tail_sem)
    tail.start()
    for k in range(TEAM):
        load((k + 1) % TEAM).start()

    barrier = pltpu.get_barrier_semaphore()
    others = [mate(k) for k in range(1, TEAM)] + [peer(k) for k in range(1, teams)]
    others += [(me + 1) % count, (me + count - 1) % count]
    for other in others:
        pl.semaphore_signal(barrier, inc=1, device_id={"ctx": other}, device_id_type=pl.DeviceIdType.MESH)

    bounds = bounds_of(lengths_ref, me * rows)
    zero_bounds = bounds_of(lengths_ref, 0)
    fill_shifts(shift_ref, bounds)
    groups = gather_ref.shape[0] // 2
    place = lax.broadcasted_iota(jnp.int32, (2 * groups, rows), 1)
    end = lax.broadcasted_iota(jnp.int32, (2 * groups, rows), 0) % groups // WIDE * BLOCK + (BLOCK - 1)
    kept = jnp.where(seg_of(place, bounds) == seg_of(end, bounds), gather_ref[...].astype(F32), 0.0).astype(BF16)
    gather_m[...] = kept
    matrix_ref[:WIDE] = kept[groups - WIDE : groups]
    matrix_ref[WIDE:] = kept[2 * groups - WIDE :]
    place = lax.broadcasted_iota(jnp.int32, block_ref.shape, 0)
    start = place // BLOCK * BLOCK
    column = lax.broadcasted_iota(jnp.int32, block_ref.shape, 1)
    source = jnp.where(column < NEAR * BLOCK, start + column % BLOCK, start - 1)
    same = seg_of(place, bounds) == seg_of(source, bounds)
    block_m[...] = jnp.where(same, block_ref[...].astype(F32), 0.0).astype(BF16)
    tail.wait()
    ends = [tail_ref[i].astype(F32)[14:16] for i in range(3)]
    packed = [e[:, :half] for e in ends] + [e[:, half:] for e in ends] + [jnp.zeros((4, half), F32)]
    edge_send[...] = jnp.concatenate(packed, axis=0).astype(BF16)

    def remote(source, target, sems, device):
        return pltpu.make_async_remote_copy(
            src_ref=source,
            dst_ref=target,
            send_sem=sems[0],
            recv_sem=sems[1],
            device_id={"ctx": device},
            device_id_type=pl.DeviceIdType.MESH,
        )

    pl.semaphore_wait(barrier, len(others))
    edge_copy = remote(edge_send, edge_land, (edge_sem.at[0], edge_sem.at[1]), (me + 1) % count)
    edge_copy.start()
    edge_copy.wait()
    landed = jnp.where(me == 0, 0.0, edge_land[...].astype(F32))
    blank = jnp.zeros((LEAD - 2, half), F32)
    for side in range(2):
        there = slice(side * half, (side + 1) * half)
        for i in range(3):
            first = 6 * side + 2 * i
            lead = jnp.concatenate([blank, landed[first : first + 2]], axis=0).astype(BF16)
            if i == 0:
                edge_ref[:, there] = lead
            else:
                rows_ref[i - 1, :LEAD, there] = lead

    def local_copy(k):
        return remote(local_send.at[k], local_land.at[k], (local_sem.at[k, 0], local_sem.at[k, 1]), mate(k))

    def one_slice(k, into):
        load(k).wait()
        base = (rank + k) % TEAM * slim

        def one_chunk(i, carry):
            here = pl.ds(pl.multiple_of(base + i * chunk, 128), chunk)
            rounded = []
            for b in range(rows // BLOCK):
                with_lead = slice(b * BLOCK, (b + 1) * BLOCK + LEAD)
                shifts = shift_ref[2 * b * BLOCK : 2 * (b + 1) * BLOCK, :]
                drive = mix(rows_ref[0, with_lead, here], taps_ref[:, 1, here], shifts) * mix(
                    rows_ref[1, with_lead, here], taps_ref[:, 2, here], shifts
                )
                drive_ref[b * BLOCK : (b + 1) * BLOCK, here] = drive
                rounded.append(drive.astype(BF16))
            moments = product_of(matrix_ref[...], jnp.concatenate(rounded, axis=0))
            moments = moments[:WIDE] + moments[WIDE:]
            rate = rate_ref[:, here]
            scale = residue_ref[:, here] * jnp.sqrt(1.0 - jnp.exp(-2.0 * rate))
            weights = lagrange(rate, nodes_of(WIDE))
            for n in range(WIDE):
                weight_ref[n, :, here] = weights[n] * scale
            state = weights[0] * moments[0:1]
            for n in range(1, WIDE):
                state = state + weights[n] * moments[n : n + 1]
            into[k, :, pl.ds(pl.multiple_of(i * chunk, 128), chunk)] = state
            return carry

        lax.fori_loop(0, slim // chunk, one_chunk, 0)

    def send_slice(k, carry):
        one_slice(k, local_send)
        local_copy(k).start()
        return carry

    lax.fori_loop(1, TEAM, send_slice, 0)
    one_slice(0, local_land)

    def out_copy(k):
        return pltpu.make_async_copy(drive_ref.at[:, span(k)], total_ref.at[:, span(k)], out_sem.at[k])

    def filter_slice(k, carry):
        base = (rank + k) % TEAM * slim

        def one_chunk(i, carry):
            here = pl.ds(pl.multiple_of(base + i * chunk, 128), chunk)
            rate = rate_ref[:, here]
            scale = residue_ref[:, here] * jnp.sqrt(1.0 - jnp.exp(-2.0 * rate))
            scale = scale * jnp.exp(F32(-MIDDLE) * rate)
            close = [jnp.sum(w * scale, axis=0, keepdims=True) for w in lagrange(rate, nodes_of(NEAR))]
            share = jnp.concatenate(
                [jnp.sum(weight_ref[n, :, here], axis=0, keepdims=True) for n in range(WIDE)], axis=0
            )
            skip = skip_ref[:, here]
            moments = product_of(gather_m[...], drive_ref[:, here].astype(BF16))
            moments = moments[:groups] + moments[groups:]
            moments = (moments.reshape(-1, WIDE, chunk) * share[None]).reshape(groups, chunk)
            high, low = halves(moments)
            for b in range(rows // BLOCK):
                span_b = slice(b * BLOCK, (b + 1) * BLOCK)
                drive = drive_ref[span_b, here]
                parts = [(c * drive).astype(BF16) for c in close]
                if b > 0:
                    before = slice((b - 1) * WIDE, b * WIDE)
                    parts += [high[before], high[before], low[before]]
                    weights = block_m[span_b, :]
                else:
                    weights = block_m[span_b, : NEAR * BLOCK]
                drive_ref[span_b, here] = skip * drive + product_of(weights, jnp.concatenate(parts, axis=0))
            return carry

        lax.fori_loop(0, slim // chunk, one_chunk, 0)
        out_copy(k).start()
        return carry

    lax.fori_loop(0, 2, filter_slice, 0)

    mine = pl.ds(pl.multiple_of(rank * slim, 128), slim)
    rate = rate_ref[:, mine]
    fade = jnp.exp(-rate * F32(rows))
    fade_team = jnp.exp(-rate * F32(rows * TEAM))

    def whole(first, devices):
        start = first * rows
        kept = seg_of(start + devices * rows - 1, zero_bounds) == seg_of(start - 1, zero_bounds)
        return kept.astype(F32)

    for k in range(1, TEAM):
        local_copy(k).wait()
    local = [local_land[(rank + TEAM - s) % TEAM] for s in range(TEAM)]
    total = local[0]
    for s in range(1, TEAM):
        total = total * (fade * whole(team * TEAM + s, 1)) + local[s]
    total_land[0] = total

    def total_copy(k):
        return remote(total_land.at[0], total_land.at[k], (total_sem.at[k, 0], total_sem.at[k, 1]), peer(k))

    for k in range(1, teams):
        total_copy(k).start()
    lax.fori_loop(2, 5, filter_slice, 0)
    for k in range(1, teams):
        total_copy(k).wait()
    state = jnp.zeros(rate.shape, F32)
    for g in range(teams - 1):
        after = state * (fade_team * whole(g * TEAM, TEAM)) + total_land[(team + teams - g) % teams]
        state = jnp.where(g < team, after, state)
    for s in range(TEAM):
        back_send[s] = state
        if s < TEAM - 1:
            state = state * (fade * whole(team * TEAM + s, 1)) + local[s]

    def back_copy(k):
        return remote(back_send.at[(rank + k) % TEAM], back_land.at[k], (back_sem.at[k, 0], back_sem.at[k, 1]), mate(k))

    for k in range(1, TEAM):
        back_copy(k).start()
    arrived_ref[:, mine] = back_send[rank]
    lax.fori_loop(5, TEAM, filter_slice, 0)
    for k in range(1, TEAM):
        back_copy(k).wait()
    for k in range(1, TEAM):
        arrived_ref[:, span(TEAM - k)] = back_land[k]

    def entry_chunk(i, carry):
        here = pl.ds(pl.multiple_of(i * chunk, 128), chunk)
        arrived = arrived_ref[:, here]
        entry_ref[:, here] = jnp.concatenate(
            [jnp.sum(weight_ref[n, :, here] * arrived, axis=0, keepdims=True) for n in range(WIDE)], axis=0
        )
        return carry

    lax.fori_loop(0, channels // chunk, entry_chunk, 0)
    for k in range(TEAM):
        out_copy(k).wait()


def output_kernel(
    fused,
    lengths_ref,
    query_ref,
    total_ref,
    edge_ref,
    taps_ref,
    gain_ref,
    entry_ref,
    arrive_ref,
    out_ref,
    square_ref,
    shift_ref,
    arrive_m,
    held_ref,
):
    rows, columns = query_ref.shape[1:]
    phase, step = pl.program_id(0), pl.program_id(1)

    @pl.when((phase == 0) & (step == 0))
    def _():
        bounds = bounds_of(lengths_ref, lax.axis_index("ctx") * rows)
        fill_shifts(shift_ref, bounds)
        square_ref[...] = jnp.zeros_like(square_ref)
        place = lax.broadcasted_iota(jnp.int32, (rows, WIDE), 0)
        same = seg_of(place, bounds) == seg_of(jnp.full((rows, WIDE), -1, jnp.int32), bounds)
        high, low = halves(jnp.where(same, arrive_ref[...], 0.0))
        arrive_m[...] = jnp.concatenate([high, low, high], axis=1)

    @pl.when(phase == 0)
    def _():
        chunk = min(CHUNK, columns)

        def one_chunk(index, carry):
            here = pl.ds(pl.multiple_of(index * chunk, 128), chunk)
            high, low = halves(entry_ref[:, here])
            entry = jnp.concatenate([high, high, low], axis=0)
            taps = taps_ref[:, 0, here]
            for b in range(rows // BLOCK):
                span_b = slice(b * BLOCK, (b + 1) * BLOCK)
                if b == 0:
                    block = jnp.concatenate([edge_ref[:, here], query_ref[0, span_b, here]], axis=0)
                else:
                    block = query_ref[0, b * BLOCK - LEAD : (b + 1) * BLOCK, here]
                query = mix(block, taps, shift_ref[2 * b * BLOCK : 2 * (b + 1) * BLOCK, :])
                response = query * (total_ref[span_b, here] + product_of(arrive_m[span_b, :], entry))
                squares = response * response
                part = squares[:, :128]
                for i in range(1, chunk // 128):
                    part = part + squares[:, i * 128 : (i + 1) * 128]
                square_ref[span_b, :] += part
                if fused:
                    held_ref[step, span_b, here] = response
                else:
                    out_ref[span_b, here] = response
            return carry

        lax.fori_loop(0, columns // chunk, one_chunk, 0)

    if fused:

        @pl.when((phase == 1) & (step == 0))
        def _():
            mean = jnp.sum(square_ref[...], axis=1, keepdims=True) / D
            square_ref[...] = jnp.broadcast_to(lax.rsqrt(mean + eps_norm), square_ref.shape)

        @pl.when(phase == 1)
        def _():
            for b in range(rows // BLOCK):
                span_b = slice(b * BLOCK, (b + 1) * BLOCK)
                scale = square_ref[span_b, :]
                for i in range(columns // 128):
                    here = slice(i * 128, (i + 1) * 128)
                    out_ref[span_b, here] = (held_ref[step, span_b, here] * scale * gain_ref[:, here]).astype(BF16)


def shards(features, short_taps, decay_rate, residue, skip_gain, norm_gain, contig_lengths):
    rows, _, channels = features.shape
    count = lax.axis_size("ctx")
    fused = lax.axis_size("chan") == 1
    poles = decay_rate.shape[0]
    planes = jnp.transpose(features, (1, 0, 2))
    columns = min(1024, channels)
    steps = channels // columns
    gather = jnp.asarray(gather_matrix(rows))
    block = jnp.asarray(block_matrix(rows))
    arrive = jnp.asarray(entry_matrix(rows), F32)
    smem = pl.BlockSpec(memory_space=pltpu.SMEM)

    vmem = pl.BlockSpec(memory_space=pltpu.VMEM)
    slim = channels // TEAM
    teams = count // TEAM
    entry, edge, total = pl.pallas_call(
        exchange_kernel,
        in_specs=[smem, pl.BlockSpec(memory_space=pl.ANY)] + [vmem] * 6,
        out_specs=[vmem, vmem, pl.BlockSpec(memory_space=pl.ANY)],
        out_shape=[
            jax.ShapeDtypeStruct((WIDE, channels), F32),
            jax.ShapeDtypeStruct((LEAD, channels), BF16),
            jax.ShapeDtypeStruct((rows, channels), F32),
        ],
        scratch_shapes=[
            pltpu.VMEM(shift_shape(rows), BF16),
            pltpu.VMEM((2 * WIDE, rows), BF16),
            pltpu.VMEM(gather.shape, BF16),
            pltpu.VMEM(block.shape, BF16),
            pltpu.VMEM((rows, channels), F32),
            pltpu.VMEM((WIDE, poles, channels), F32),
            pltpu.VMEM((poles, channels), F32),
            pltpu.VMEM((2, LEAD + rows, channels), BF16),
            pltpu.VMEM((3, 16, channels), BF16),
            pltpu.VMEM((16, channels // 2), BF16),
            pltpu.VMEM((16, channels // 2), BF16),
            pltpu.VMEM((TEAM, poles, slim), F32),
            pltpu.VMEM((TEAM, poles, slim), F32),
            pltpu.VMEM((teams, poles, slim), F32),
            pltpu.VMEM((TEAM, poles, slim), F32),
            pltpu.VMEM((TEAM, poles, slim), F32),
            pltpu.SemaphoreType.DMA((TEAM,)),
            pltpu.SemaphoreType.DMA,
            pltpu.SemaphoreType.DMA((2,)),
            pltpu.SemaphoreType.DMA((TEAM, 2)),
            pltpu.SemaphoreType.DMA((teams, 2)),
            pltpu.SemaphoreType.DMA((TEAM, 2)),
            pltpu.SemaphoreType.DMA((TEAM,)),
        ],
        compiler_params=pltpu.CompilerParams(
            collective_id=0, has_side_effects=True, vmem_limit_bytes=60 << 20
        ),
        name="exchange",
    )(
        contig_lengths,
        planes,
        short_taps,
        decay_rate,
        residue,
        skip_gain.reshape(1, channels),
        gather,
        block,
    )

    def at(phase, j):
        return jnp.where(phase == 0, j, steps - 1)

    def per_block(shape):
        lead = (0,) * (len(shape) - 1)
        return pl.BlockSpec(shape, lambda phase, j: lead + (at(phase, j),))

    def plane_two(i):
        return pl.BlockSpec((1, rows, columns), lambda phase, j: (i, 0, at(phase, j)))

    def still(array):
        return pl.BlockSpec(array.shape, lambda phase, j: (0,) * array.ndim)

    if fused:
        out_map = lambda phase, j: (0, jnp.where(phase == 0, 0, j))
    else:
        out_map = lambda phase, j: (0, j)
    result, squares = pl.pallas_call(
        functools.partial(output_kernel, fused),
        grid=(2 if fused else 1, steps),
        in_specs=[
            smem,
            plane_two(0),
            per_block((rows, columns)),
            per_block((LEAD, columns)),
            per_block((3, 3, columns)),
            pl.BlockSpec((1, columns), lambda phase, j: (0, j)),
            per_block((WIDE, columns)),
            still(arrive),
        ],
        out_specs=[pl.BlockSpec((rows, columns), out_map), pl.BlockSpec((rows, 128), lambda phase, j: (0, 0))],
        out_shape=[
            jax.ShapeDtypeStruct((rows, channels), BF16 if fused else F32),
            jax.ShapeDtypeStruct((rows, 128), F32),
        ],
        scratch_shapes=[
            pltpu.VMEM(shift_shape(rows), BF16),
            pltpu.VMEM((rows, 3 * WIDE), BF16),
            pltpu.VMEM((steps, rows, columns) if fused else (1, 8, 128), F32),
        ],
        compiler_params=pltpu.CompilerParams(vmem_limit_bytes=60 << 20),
        name="output",
    )(contig_lengths, planes, total, edge, short_taps, norm_gain.reshape(1, channels), entry, arrive)
    if fused:
        return result
    mean = lax.psum(jnp.sum(squares, axis=1, keepdims=True), "chan") / D
    return (result * lax.rsqrt(mean + eps_norm) * norm_gain[None, :]).astype(BF16)


def solution(mesh):
    placed = (
        P("ctx", None, "chan"),
        P(None, None, "chan"),
        P(None, "chan"),
        P(None, "chan"),
        P("chan"),
        P("chan"),
        P(),
    )
    return jax.shard_map(
        shards, mesh=mesh, in_specs=placed, out_specs=P("ctx", "chan"), check_vma=False
    )
```

```python
import functools

import jax
import jax.numpy as jnp
import ml_dtypes
import numpy as np
from jax import lax
from jax.experimental import pallas as pl
from jax.experimental.pallas import tpu as pltpu
from jax.sharding import PartitionSpec as P

D = 8192
eps_norm = 1e-05
RATE_TOP = 1.0 / 30.0 * (1.0 + 1e-6)
BLOCK = 32
WIDE = 16
NEAR = 6
MIDDLE = (BLOCK - 1) / 2
TEAM = 8
LEAD = 16
CHUNK = 512
F32 = jnp.float32
BF16 = jnp.bfloat16


def nodes_of(count):
    angle = (2 * np.arange(count) + 1) * np.pi / (2 * count)
    return RATE_TOP / 2 * (1 - np.cos(angle))


def lagrange(rate, nodes):
    count = len(nodes)
    unit = nodes / RATE_TOP
    scaled = rate * F32(1.0 / RATE_TOP)
    gaps = [scaled - F32(u) for u in unit]
    ahead = [None] * count
    for i in range(1, count):
        ahead[i] = gaps[i - 1] if i == 1 else ahead[i - 1] * gaps[i - 1]
    weights = [None] * count
    after = None
    for i in reversed(range(count)):
        norm = F32(1.0 / np.prod([unit[i] - unit[j] for j in range(count) if j != i]))
        if after is None:
            weights[i] = ahead[i] * norm
            after = gaps[i]
        else:
            weights[i] = (after if i == 0 else ahead[i] * after) * norm
            after = after * gaps[i]
    return weights


def split(matrix):
    high = matrix.astype(ml_dtypes.bfloat16)
    return high, (matrix - high.astype(np.float64)).astype(ml_dtypes.bfloat16)


def gather_matrix(rows):
    nodes = nodes_of(WIDE)
    index = np.arange(rows // BLOCK * WIDE)
    end = (index // WIDE + 1) * BLOCK - 1
    lag = end[:, None] - np.arange(rows)[None, :]
    matrix = np.where(lag >= 0, np.exp(-nodes[index % WIDE][:, None] * np.maximum(lag, 0)), 0.0)
    return np.concatenate(split(matrix), axis=0)


def block_matrix(rows):
    place = np.arange(rows)[:, None] % BLOCK
    lag = place - np.arange(BLOCK)[None, :]
    near = [np.where(lag >= 0, np.exp(-node * (lag - MIDDLE)), 0.0) for node in nodes_of(NEAR)]
    high, low = split(np.exp(-nodes_of(WIDE)[None, :] * (place + 1.0)))
    return np.concatenate([split(n)[0] for n in near] + [high, low, high], axis=1)


def entry_matrix(rows):
    return np.exp(-nodes_of(WIDE)[None, :] * (np.arange(rows)[:, None] + 1.0))


def near_matrices(rows):
    lag = np.arange(rows)[:, None] - np.arange(rows)[None, :]
    same = (np.arange(rows)[:, None] // BLOCK == np.arange(rows)[None, :] // BLOCK) & (lag >= 0)
    return np.stack(
        [np.where(same, np.exp(-node * np.maximum(lag, 0)), 0.0) for node in nodes_of(NEAR)]
    )


def bounds_of(lengths_ref, anchor):
    total = -anchor
    bounds = []
    for i in range(lengths_ref.shape[0] - 1):
        total = total + lengths_ref[i]
        bounds.append(total)
    return bounds


def seg_of(place, bounds):
    return sum((place >= b).astype(jnp.int32) for b in bounds)


def halves(value):
    high = value.astype(BF16)
    return high, (value - high.astype(F32)).astype(BF16)


def product_of(left, right):
    return jnp.dot(left, right, preferred_element_type=F32)


def wide(column, columns):
    return jnp.concatenate([column] * (columns // column.shape[1]), axis=1)


def shift_shape(rows):
    return (2 * rows, BLOCK + LEAD)


def fill_shifts(shift_ref, bounds):
    down = lax.broadcasted_iota(jnp.int32, shift_ref.shape, 0)
    column = lax.broadcasted_iota(jnp.int32, shift_ref.shape, 1)
    by = 1 + down % (2 * BLOCK) // BLOCK
    place = down // (2 * BLOCK) * BLOCK + down % BLOCK
    same = seg_of(place, bounds) == seg_of(place - by, bounds)
    used = same & (column == LEAD + down % BLOCK - by)
    shift_ref[...] = jnp.where(used, 1.0, 0.0).astype(BF16)


def mix(block, taps, shifts):
    moved = product_of(shifts, block)
    now = block[LEAD:].astype(F32)
    return taps[0:1] * now + taps[1:2] * moved[:BLOCK] + taps[2:3] * moved[BLOCK:]


def exchange_kernel(
    lengths_ref,
    planes_ref,
    taps_ref,
    rate_ref,
    residue_ref,
    skip_ref,
    gather_ref,
    block_ref,
    entry_ref,
    edge_ref,
    total_ref,
    shift_ref,
    matrix_ref,
    gather_m,
    block_m,
    drive_ref,
    weight_ref,
    arrived_ref,
    rows_ref,
    tail_ref,
    edge_send,
    edge_land,
    local_send,
    local_land,
    total_land,
    back_send,
    back_land,
    rows_sem,
    tail_sem,
    edge_sem,
    local_sem,
    total_sem,
    back_sem,
    out_sem,
):
    rows, channels = planes_ref.shape[1:]
    half = channels // 2
    count = lax.axis_size("ctx")
    teams = count // TEAM
    slim = channels // TEAM
    chunk = min(CHUNK, slim)
    me = lax.axis_index("ctx")
    team, rank = me // TEAM, me % TEAM

    def mate(k):
        return team * TEAM + (rank + k) % TEAM

    def peer(k):
        return (team + k) % teams * TEAM + rank

    def span(k):
        return pl.ds(pl.multiple_of((rank + k) % TEAM * slim, 128), slim)

    def load(k):
        return pltpu.make_async_copy(
            planes_ref.at[pl.ds(1, 2), :, span(k)], rows_ref.at[:, pl.ds(LEAD, rows), span(k)], rows_sem.at[k]
        )

    tail = pltpu.make_async_copy(planes_ref.at[:, pl.ds(rows - 16, 16), :], tail_ref, tail_sem)
    tail.start()
    for k in range(TEAM):
        load((k + 1) % TEAM).start()

    barrier = pltpu.get_barrier_semaphore()
    others = [mate(k) for k in range(1, TEAM)] + [peer(k) for k in range(1, teams)]
    others += [(me + 1) % count, (me + count - 1) % count]
    for other in others:
        pl.semaphore_signal(barrier, inc=1, device_id={"ctx": other}, device_id_type=pl.DeviceIdType.MESH)

    bounds = bounds_of(lengths_ref, me * rows)
    zero_bounds = bounds_of(lengths_ref, 0)
    fill_shifts(shift_ref, bounds)
    groups = gather_ref.shape[0] // 2
    place = lax.broadcasted_iota(jnp.int32, (2 * groups, rows), 1)
    end = lax.broadcasted_iota(jnp.int32, (2 * groups, rows), 0) % groups // WIDE * BLOCK + (BLOCK - 1)
    kept = jnp.where(seg_of(place, bounds) == seg_of(end, bounds), gather_ref[...].astype(F32), 0.0).astype(BF16)
    gather_m[...] = kept
    matrix_ref[:WIDE] = kept[groups - WIDE : groups]
    matrix_ref[WIDE:] = kept[2 * groups - WIDE :]
    place = lax.broadcasted_iota(jnp.int32, block_ref.shape, 0)
    start = place // BLOCK * BLOCK
    column = lax.broadcasted_iota(jnp.int32, block_ref.shape, 1)
    source = jnp.where(column < NEAR * BLOCK, start + column % BLOCK, start - 1)
    same = seg_of(place, bounds) == seg_of(source, bounds)
    block_m[...] = jnp.where(same, block_ref[...].astype(F32), 0.0).astype(BF16)
    tail.wait()
    ends = [tail_ref[i].astype(F32)[14:16] for i in range(3)]
    packed = [e[:, :half] for e in ends] + [e[:, half:] for e in ends] + [jnp.zeros((4, half), F32)]
    edge_send[...] = jnp.concatenate(packed, axis=0).astype(BF16)

    def remote(source, target, sems, device):
        return pltpu.make_async_remote_copy(
            src_ref=source,
            dst_ref=target,
            send_sem=sems[0],
            recv_sem=sems[1],
            device_id={"ctx": device},
            device_id_type=pl.DeviceIdType.MESH,
        )

    pl.semaphore_wait(barrier, len(others))
    edge_copy = remote(edge_send, edge_land, (edge_sem.at[0], edge_sem.at[1]), (me + 1) % count)
    edge_copy.start()
    edge_copy.wait()
    landed = jnp.where(me == 0, 0.0, edge_land[...].astype(F32))
    blank = jnp.zeros((LEAD - 2, half), F32)
    for side in range(2):
        there = slice(side * half, (side + 1) * half)
        for i in range(3):
            first = 6 * side + 2 * i
            lead = jnp.concatenate([blank, landed[first : first + 2]], axis=0).astype(BF16)
            if i == 0:
                edge_ref[:, there] = lead
            else:
                rows_ref[i - 1, :LEAD, there] = lead

    def local_copy(k):
        return remote(local_send.at[k], local_land.at[k], (local_sem.at[k, 0], local_sem.at[k, 1]), mate(k))

    def one_slice(k, into):
        load(k).wait()
        base = (rank + k) % TEAM * slim

        def one_chunk(i, carry):
            here = pl.ds(pl.multiple_of(base + i * chunk, 128), chunk)
            rounded = []
            for b in range(rows // BLOCK):
                with_lead = slice(b * BLOCK, (b + 1) * BLOCK + LEAD)
                shifts = shift_ref[2 * b * BLOCK : 2 * (b + 1) * BLOCK, :]
                drive = mix(rows_ref[0, with_lead, here], taps_ref[:, 1, here], shifts) * mix(
                    rows_ref[1, with_lead, here], taps_ref[:, 2, here], shifts
                )
                drive_ref[b * BLOCK : (b + 1) * BLOCK, here] = drive
                rounded.append(drive.astype(BF16))
            moments = product_of(matrix_ref[...], jnp.concatenate(rounded, axis=0))
            moments = moments[:WIDE] + moments[WIDE:]
            rate = rate_ref[:, here]
            scale = residue_ref[:, here] * jnp.sqrt(1.0 - jnp.exp(-2.0 * rate))
            weights = lagrange(rate, nodes_of(WIDE))
            for n in range(WIDE):
                weight_ref[n, :, here] = weights[n] * scale
            state = weights[0] * moments[0:1]
            for n in range(1, WIDE):
                state = state + weights[n] * moments[n : n + 1]
            into[k, :, pl.ds(pl.multiple_of(i * chunk, 128), chunk)] = state
            return carry

        lax.fori_loop(0, slim // chunk, one_chunk, 0)

    def send_slice(k, carry):
        one_slice(k, local_send)
        local_copy(k).start()
        return carry

    lax.fori_loop(1, TEAM, send_slice, 0)
    one_slice(0, local_land)

    def out_copy(k):
        return pltpu.make_async_copy(drive_ref.at[:, span(k)], total_ref.at[:, span(k)], out_sem.at[k])

    def filter_slice(k, carry):
        base = (rank + k) % TEAM * slim

        def one_chunk(i, carry):
            here = pl.ds(pl.multiple_of(base + i * chunk, 128), chunk)
            rate = rate_ref[:, here]
            scale = residue_ref[:, here] * jnp.sqrt(1.0 - jnp.exp(-2.0 * rate))
            scale = scale * jnp.exp(F32(-MIDDLE) * rate)
            close = [jnp.sum(w * scale, axis=0, keepdims=True) for w in lagrange(rate, nodes_of(NEAR))]
            share = jnp.concatenate(
                [jnp.sum(weight_ref[n, :, here], axis=0, keepdims=True) for n in range(WIDE)], axis=0
            )
            skip = skip_ref[:, here]
            moments = product_of(gather_m[...], drive_ref[:, here].astype(BF16))
            moments = moments[:groups] + moments[groups:]
            moments = (moments.reshape(-1, WIDE, chunk) * share[None]).reshape(groups, chunk)
            high, low = halves(moments)
            for b in range(rows // BLOCK):
                span_b = slice(b * BLOCK, (b + 1) * BLOCK)
                drive = drive_ref[span_b, here]
                parts = [(c * drive).astype(BF16) for c in close]
                if b > 0:
                    before = slice((b - 1) * WIDE, b * WIDE)
                    parts += [high[before], high[before], low[before]]
                    weights = block_m[span_b, :]
                else:
                    weights = block_m[span_b, : NEAR * BLOCK]
                drive_ref[span_b, here] = skip * drive + product_of(weights, jnp.concatenate(parts, axis=0))
            return carry

        lax.fori_loop(0, slim // chunk, one_chunk, 0)
        out_copy(k).start()
        return carry

    lax.fori_loop(0, 2, filter_slice, 0)

    mine = pl.ds(pl.multiple_of(rank * slim, 128), slim)
    rate = rate_ref[:, mine]
    fade = jnp.exp(-rate * F32(rows))
    fade_team = jnp.exp(-rate * F32(rows * TEAM))

    def whole(first, devices):
        start = first * rows
        kept = seg_of(start + devices * rows - 1, zero_bounds) == seg_of(start - 1, zero_bounds)
        return kept.astype(F32)

    for k in range(1, TEAM):
        local_copy(k).wait()
    local = [local_land[(rank + TEAM - s) % TEAM] for s in range(TEAM)]
    total = local[0]
    for s in range(1, TEAM):
        total = total * (fade * whole(team * TEAM + s, 1)) + local[s]
    total_land[0] = total

    def total_copy(k):
        return remote(total_land.at[0], total_land.at[k], (total_sem.at[k, 0], total_sem.at[k, 1]), peer(k))

    for k in range(1, teams):
        total_copy(k).start()
    lax.fori_loop(2, 5, filter_slice, 0)
    for k in range(1, teams):
        total_copy(k).wait()
    state = jnp.zeros(rate.shape, F32)
    for g in range(teams - 1):
        after = state * (fade_team * whole(g * TEAM, TEAM)) + total_land[(team + teams - g) % teams]
        state = jnp.where(g < team, after, state)
    for s in range(TEAM):
        back_send[s] = state
        if s < TEAM - 1:
            state = state * (fade * whole(team * TEAM + s, 1)) + local[s]

    def back_copy(k):
        return remote(back_send.at[(rank + k) % TEAM], back_land.at[k], (back_sem.at[k, 0], back_sem.at[k, 1]), mate(k))

    for k in range(1, TEAM):
        back_copy(k).start()
    arrived_ref[:, mine] = back_send[rank]
    lax.fori_loop(5, TEAM, filter_slice, 0)
    for k in range(1, TEAM):
        back_copy(k).wait()
    for k in range(1, TEAM):
        arrived_ref[:, span(TEAM - k)] = back_land[k]

    def entry_chunk(i, carry):
        here = pl.ds(pl.multiple_of(i * chunk, 128), chunk)
        arrived = arrived_ref[:, here]
        entry_ref[:, here] = jnp.concatenate(
            [jnp.sum(weight_ref[n, :, here] * arrived, axis=0, keepdims=True) for n in range(WIDE)], axis=0
        )
        return carry

    lax.fori_loop(0, channels // chunk, entry_chunk, 0)
    for k in range(TEAM):
        out_copy(k).wait()


def output_kernel(
    fused,
    lengths_ref,
    query_ref,
    total_ref,
    edge_ref,
    taps_ref,
    gain_ref,
    entry_ref,
    arrive_ref,
    out_ref,
    square_ref,
    shift_ref,
    arrive_m,
    held_ref,
):
    rows, columns = query_ref.shape[1:]
    phase, step = pl.program_id(0), pl.program_id(1)

    @pl.when((phase == 0) & (step == 0))
    def _():
        bounds = bounds_of(lengths_ref, lax.axis_index("ctx") * rows)
        fill_shifts(shift_ref, bounds)
        square_ref[...] = jnp.zeros_like(square_ref)
        place = lax.broadcasted_iota(jnp.int32, (rows, WIDE), 0)
        same = seg_of(place, bounds) == seg_of(jnp.full((rows, WIDE), -1, jnp.int32), bounds)
        high, low = halves(jnp.where(same, arrive_ref[...], 0.0))
        arrive_m[...] = jnp.concatenate([high, low, high], axis=1)

    @pl.when(phase == 0)
    def _():
        chunk = min(CHUNK, columns)

        def one_chunk(index, carry):
            here = pl.ds(pl.multiple_of(index * chunk, 128), chunk)
            high, low = halves(entry_ref[:, here])
            entry = jnp.concatenate([high, high, low], axis=0)
            taps = taps_ref[:, 0, here]
            for b in range(rows // BLOCK):
                span_b = slice(b * BLOCK, (b + 1) * BLOCK)
                if b == 0:
                    block = jnp.concatenate([edge_ref[:, here], query_ref[0, span_b, here]], axis=0)
                else:
                    block = query_ref[0, b * BLOCK - LEAD : (b + 1) * BLOCK, here]
                query = mix(block, taps, shift_ref[2 * b * BLOCK : 2 * (b + 1) * BLOCK, :])
                response = query * (total_ref[span_b, here] + product_of(arrive_m[span_b, :], entry))
                squares = response * response
                part = squares[:, :128]
                for i in range(1, chunk // 128):
                    part = part + squares[:, i * 128 : (i + 1) * 128]
                square_ref[span_b, :] += part
                if fused:
                    held_ref[step, span_b, here] = response
                else:
                    out_ref[span_b, here] = response
            return carry

        lax.fori_loop(0, columns // chunk, one_chunk, 0)

    if fused:

        @pl.when((phase == 1) & (step == 0))
        def _():
            mean = jnp.sum(square_ref[...], axis=1, keepdims=True) / D
            square_ref[...] = jnp.broadcast_to(lax.rsqrt(mean + eps_norm), square_ref.shape)

        @pl.when(phase == 1)
        def _():
            for b in range(rows // BLOCK):
                span_b = slice(b * BLOCK, (b + 1) * BLOCK)
                scale = square_ref[span_b, :]
                for i in range(columns // 128):
                    here = slice(i * 128, (i + 1) * 128)
                    out_ref[span_b, here] = (held_ref[step, span_b, here] * scale * gain_ref[:, here]).astype(BF16)


def shards(features, short_taps, decay_rate, residue, skip_gain, norm_gain, contig_lengths):
    rows, _, channels = features.shape
    count = lax.axis_size("ctx")
    fused = lax.axis_size("chan") == 1
    poles = decay_rate.shape[0]
    planes = jnp.transpose(features, (1, 0, 2))
    columns = min(2048, channels)
    steps = channels // columns
    gather = jnp.asarray(gather_matrix(rows))
    block = jnp.asarray(block_matrix(rows))
    arrive = jnp.asarray(entry_matrix(rows), F32)
    smem = pl.BlockSpec(memory_space=pltpu.SMEM)

    vmem = pl.BlockSpec(memory_space=pltpu.VMEM)
    slim = channels // TEAM
    teams = count // TEAM
    entry, edge, total = pl.pallas_call(
        exchange_kernel,
        in_specs=[smem, pl.BlockSpec(memory_space=pl.ANY)] + [vmem] * 6,
        out_specs=[vmem, vmem, pl.BlockSpec(memory_space=pl.ANY)],
        out_shape=[
            jax.ShapeDtypeStruct((WIDE, channels), F32),
            jax.ShapeDtypeStruct((LEAD, channels), BF16),
            jax.ShapeDtypeStruct((rows, channels), F32),
        ],
        scratch_shapes=[
            pltpu.VMEM(shift_shape(rows), BF16),
            pltpu.VMEM((2 * WIDE, rows), BF16),
            pltpu.VMEM(gather.shape, BF16),
            pltpu.VMEM(block.shape, BF16),
            pltpu.VMEM((rows, channels), F32),
            pltpu.VMEM((WIDE, poles, channels), F32),
            pltpu.VMEM((poles, channels), F32),
            pltpu.VMEM((2, LEAD + rows, channels), BF16),
            pltpu.VMEM((3, 16, channels), BF16),
            pltpu.VMEM((16, channels // 2), BF16),
            pltpu.VMEM((16, channels // 2), BF16),
            pltpu.VMEM((TEAM, poles, slim), F32),
            pltpu.VMEM((TEAM, poles, slim), F32),
            pltpu.VMEM((teams, poles, slim), F32),
            pltpu.VMEM((TEAM, poles, slim), F32),
            pltpu.VMEM((TEAM, poles, slim), F32),
            pltpu.SemaphoreType.DMA((TEAM,)),
            pltpu.SemaphoreType.DMA,
            pltpu.SemaphoreType.DMA((2,)),
            pltpu.SemaphoreType.DMA((TEAM, 2)),
            pltpu.SemaphoreType.DMA((teams, 2)),
            pltpu.SemaphoreType.DMA((TEAM, 2)),
            pltpu.SemaphoreType.DMA((TEAM,)),
        ],
        compiler_params=pltpu.CompilerParams(
            collective_id=0, has_side_effects=True, vmem_limit_bytes=60 << 20
        ),
        name="exchange",
    )(
        contig_lengths,
        planes,
        short_taps,
        decay_rate,
        residue,
        skip_gain.reshape(1, channels),
        gather,
        block,
    )

    def at(phase, j):
        return jnp.where(phase == 0, j, steps - 1)

    def per_block(shape):
        lead = (0,) * (len(shape) - 1)
        return pl.BlockSpec(shape, lambda phase, j: lead + (at(phase, j),))

    def plane_two(i):
        return pl.BlockSpec((1, rows, columns), lambda phase, j: (i, 0, at(phase, j)))

    def still(array):
        return pl.BlockSpec(array.shape, lambda phase, j: (0,) * array.ndim)

    if fused:
        out_map = lambda phase, j: (0, jnp.where(phase == 0, 0, j))
    else:
        out_map = lambda phase, j: (0, j)
    result, squares = pl.pallas_call(
        functools.partial(output_kernel, fused),
        grid=(2 if fused else 1, steps),
        in_specs=[
            smem,
            plane_two(0),
            per_block((rows, columns)),
            per_block((LEAD, columns)),
            per_block((3, 3, columns)),
            pl.BlockSpec((1, columns), lambda phase, j: (0, j)),
            per_block((WIDE, columns)),
            still(arrive),
        ],
        out_specs=[pl.BlockSpec((rows, columns), out_map), pl.BlockSpec((rows, 128), lambda phase, j: (0, 0))],
        out_shape=[
            jax.ShapeDtypeStruct((rows, channels), BF16 if fused else F32),
            jax.ShapeDtypeStruct((rows, 128), F32),
        ],
        scratch_shapes=[
            pltpu.VMEM(shift_shape(rows), BF16),
            pltpu.VMEM((rows, 3 * WIDE), BF16),
            pltpu.VMEM((steps, rows, columns) if fused else (1, 8, 128), F32),
        ],
        compiler_params=pltpu.CompilerParams(vmem_limit_bytes=60 << 20),
        name="output",
    )(contig_lengths, planes, total, edge, short_taps, norm_gain.reshape(1, channels), entry, arrive)
    if fused:
        return result
    mean = lax.psum(jnp.sum(squares, axis=1, keepdims=True), "chan") / D
    return (result * lax.rsqrt(mean + eps_norm) * norm_gain[None, :]).astype(BF16)


def solution(mesh):
    placed = (
        P("ctx", None, "chan"),
        P(None, None, "chan"),
        P(None, "chan"),
        P(None, "chan"),
        P("chan"),
        P("chan"),
        P(),
    )
    return jax.shard_map(
        shards, mesh=mesh, in_specs=placed, out_specs=P("ctx", "chan"), check_vma=False
    )
```

```python
import functools

import jax
import jax.numpy as jnp
import ml_dtypes
import numpy as np
from jax import lax
from jax.experimental import pallas as pl
from jax.experimental.pallas import tpu as pltpu
from jax.sharding import PartitionSpec as P

D = 8192
eps_norm = 1e-05
RATE_TOP = 1.0 / 30.0 * (1.0 + 1e-6)
BLOCK = 32
WIDE = 16
NEAR = 6
MIDDLE = (BLOCK - 1) / 2
TEAM = 8
LEAD = 16
CHUNK = 1024
F32 = jnp.float32
BF16 = jnp.bfloat16


def nodes_of(count):
    angle = (2 * np.arange(count) + 1) * np.pi / (2 * count)
    return RATE_TOP / 2 * (1 - np.cos(angle))


def lagrange(rate, nodes):
    count = len(nodes)
    unit = nodes / RATE_TOP
    scaled = rate * F32(1.0 / RATE_TOP)
    gaps = [scaled - F32(u) for u in unit]
    ahead = [None] * count
    for i in range(1, count):
        ahead[i] = gaps[i - 1] if i == 1 else ahead[i - 1] * gaps[i - 1]
    weights = [None] * count
    after = None
    for i in reversed(range(count)):
        norm = F32(1.0 / np.prod([unit[i] - unit[j] for j in range(count) if j != i]))
        if after is None:
            weights[i] = ahead[i] * norm
            after = gaps[i]
        else:
            weights[i] = (after if i == 0 else ahead[i] * after) * norm
            after = after * gaps[i]
    return weights


def split(matrix):
    high = matrix.astype(ml_dtypes.bfloat16)
    return high, (matrix - high.astype(np.float64)).astype(ml_dtypes.bfloat16)


def gather_matrix(rows):
    nodes = nodes_of(WIDE)
    index = np.arange(rows // BLOCK * WIDE)
    end = (index // WIDE + 1) * BLOCK - 1
    lag = end[:, None] - np.arange(rows)[None, :]
    matrix = np.where(lag >= 0, np.exp(-nodes[index % WIDE][:, None] * np.maximum(lag, 0)), 0.0)
    return np.concatenate(split(matrix), axis=0)


def block_matrix(rows):
    place = np.arange(rows)[:, None] % BLOCK
    lag = place - np.arange(BLOCK)[None, :]
    near = [np.where(lag >= 0, np.exp(-node * (lag - MIDDLE)), 0.0) for node in nodes_of(NEAR)]
    high, low = split(np.exp(-nodes_of(WIDE)[None, :] * (place + 1.0)))
    return np.concatenate([split(n)[0] for n in near] + [high, low, high], axis=1)


def entry_matrix(rows):
    return np.exp(-nodes_of(WIDE)[None, :] * (np.arange(rows)[:, None] + 1.0))


def near_matrices(rows):
    lag = np.arange(rows)[:, None] - np.arange(rows)[None, :]
    same = (np.arange(rows)[:, None] // BLOCK == np.arange(rows)[None, :] // BLOCK) & (lag >= 0)
    return np.stack(
        [np.where(same, np.exp(-node * np.maximum(lag, 0)), 0.0) for node in nodes_of(NEAR)]
    )


def bounds_of(lengths_ref, anchor):
    total = -anchor
    bounds = []
    for i in range(lengths_ref.shape[0] - 1):
        total = total + lengths_ref[i]
        bounds.append(total)
    return bounds


def seg_of(place, bounds):
    return sum((place >= b).astype(jnp.int32) for b in bounds)


def halves(value):
    high = value.astype(BF16)
    return high, (value - high.astype(F32)).astype(BF16)


def product_of(left, right):
    return jnp.dot(left, right, preferred_element_type=F32)


def wide(column, columns):
    return jnp.concatenate([column] * (columns // column.shape[1]), axis=1)


def shift_shape(rows):
    return (2 * rows, BLOCK + LEAD)


def fill_shifts(shift_ref, bounds):
    down = lax.broadcasted_iota(jnp.int32, shift_ref.shape, 0)
    column = lax.broadcasted_iota(jnp.int32, shift_ref.shape, 1)
    by = 1 + down % (2 * BLOCK) // BLOCK
    place = down // (2 * BLOCK) * BLOCK + down % BLOCK
    same = seg_of(place, bounds) == seg_of(place - by, bounds)
    used = same & (column == LEAD + down % BLOCK - by)
    shift_ref[...] = jnp.where(used, 1.0, 0.0).astype(BF16)


def mix(block, taps, shifts):
    moved = product_of(shifts, block)
    now = block[LEAD:].astype(F32)
    return taps[0:1] * now + taps[1:2] * moved[:BLOCK] + taps[2:3] * moved[BLOCK:]


def exchange_kernel(
    lengths_ref,
    planes_ref,
    taps_ref,
    rate_ref,
    residue_ref,
    skip_ref,
    gather_ref,
    block_ref,
    entry_ref,
    edge_ref,
    total_ref,
    shift_ref,
    matrix_ref,
    gather_m,
    block_m,
    drive_ref,
    weight_ref,
    arrived_ref,
    rows_ref,
    tail_ref,
    edge_send,
    edge_land,
    local_send,
    local_land,
    total_land,
    back_send,
    back_land,
    rows_sem,
    tail_sem,
    edge_sem,
    local_sem,
    total_sem,
    back_sem,
    out_sem,
):
    rows, channels = planes_ref.shape[1:]
    half = channels // 2
    count = lax.axis_size("ctx")
    teams = count // TEAM
    slim = channels // TEAM
    chunk = min(CHUNK, slim)
    me = lax.axis_index("ctx")
    team, rank = me // TEAM, me % TEAM

    def mate(k):
        return team * TEAM + (rank + k) % TEAM

    def peer(k):
        return (team + k) % teams * TEAM + rank

    def span(k):
        return pl.ds(pl.multiple_of((rank + k) % TEAM * slim, 128), slim)

    def load(k):
        return pltpu.make_async_copy(
            planes_ref.at[pl.ds(1, 2), :, span(k)], rows_ref.at[:, pl.ds(LEAD, rows), span(k)], rows_sem.at[k]
        )

    tail = pltpu.make_async_copy(planes_ref.at[:, pl.ds(rows - 16, 16), :], tail_ref, tail_sem)
    tail.start()
    for k in range(TEAM):
        load((k + 1) % TEAM).start()

    barrier = pltpu.get_barrier_semaphore()
    others = [mate(k) for k in range(1, TEAM)] + [peer(k) for k in range(1, teams)]
    others += [(me + 1) % count, (me + count - 1) % count]
    for other in others:
        pl.semaphore_signal(barrier, inc=1, device_id={"ctx": other}, device_id_type=pl.DeviceIdType.MESH)

    bounds = bounds_of(lengths_ref, me * rows)
    zero_bounds = bounds_of(lengths_ref, 0)
    fill_shifts(shift_ref, bounds)
    groups = gather_ref.shape[0] // 2
    place = lax.broadcasted_iota(jnp.int32, (2 * groups, rows), 1)
    end = lax.broadcasted_iota(jnp.int32, (2 * groups, rows), 0) % groups // WIDE * BLOCK + (BLOCK - 1)
    kept = jnp.where(seg_of(place, bounds) == seg_of(end, bounds), gather_ref[...].astype(F32), 0.0).astype(BF16)
    gather_m[...] = kept
    matrix_ref[:WIDE] = kept[groups - WIDE : groups]
    matrix_ref[WIDE:] = kept[2 * groups - WIDE :]
    place = lax.broadcasted_iota(jnp.int32, block_ref.shape, 0)
    start = place // BLOCK * BLOCK
    column = lax.broadcasted_iota(jnp.int32, block_ref.shape, 1)
    source = jnp.where(column < NEAR * BLOCK, start + column % BLOCK, start - 1)
    same = seg_of(place, bounds) == seg_of(source, bounds)
    block_m[...] = jnp.where(same, block_ref[...].astype(F32), 0.0).astype(BF16)
    tail.wait()
    ends = [tail_ref[i].astype(F32)[14:16] for i in range(3)]
    packed = [e[:, :half] for e in ends] + [e[:, half:] for e in ends] + [jnp.zeros((4, half), F32)]
    edge_send[...] = jnp.concatenate(packed, axis=0).astype(BF16)

    def remote(source, target, sems, device):
        return pltpu.make_async_remote_copy(
            src_ref=source,
            dst_ref=target,
            send_sem=sems[0],
            recv_sem=sems[1],
            device_id={"ctx": device},
            device_id_type=pl.DeviceIdType.MESH,
        )

    pl.semaphore_wait(barrier, len(others))
    edge_copy = remote(edge_send, edge_land, (edge_sem.at[0], edge_sem.at[1]), (me + 1) % count)
    edge_copy.start()
    edge_copy.wait()
    landed = jnp.where(me == 0, 0.0, edge_land[...].astype(F32))
    blank = jnp.zeros((LEAD - 2, half), F32)
    for side in range(2):
        there = slice(side * half, (side + 1) * half)
        for i in range(3):
            first = 6 * side + 2 * i
            lead = jnp.concatenate([blank, landed[first : first + 2]], axis=0).astype(BF16)
            if i == 0:
                edge_ref[:, there] = lead
            else:
                rows_ref[i - 1, :LEAD, there] = lead

    def local_copy(k):
        return remote(local_send.at[k], local_land.at[k], (local_sem.at[k, 0], local_sem.at[k, 1]), mate(k))

    def one_slice(k, into):
        load(k).wait()
        base = (rank + k) % TEAM * slim

        def one_chunk(i, carry):
            here = pl.ds(pl.multiple_of(base + i * chunk, 128), chunk)
            rounded = []
            for b in range(rows // BLOCK):
                with_lead = slice(b * BLOCK, (b + 1) * BLOCK + LEAD)
                shifts = shift_ref[2 * b * BLOCK : 2 * (b + 1) * BLOCK, :]
                drive = mix(rows_ref[0, with_lead, here], taps_ref[:, 1, here], shifts) * mix(
                    rows_ref[1, with_lead, here], taps_ref[:, 2, here], shifts
                )
                drive_ref[b * BLOCK : (b + 1) * BLOCK, here] = drive
                rounded.append(drive.astype(BF16))
            moments = product_of(matrix_ref[...], jnp.concatenate(rounded, axis=0))
            moments = moments[:WIDE] + moments[WIDE:]
            rate = rate_ref[:, here]
            scale = residue_ref[:, here] * jnp.sqrt(1.0 - jnp.exp(-2.0 * rate))
            weights = lagrange(rate, nodes_of(WIDE))
            for n in range(WIDE):
                weight_ref[n, :, here] = weights[n] * scale
            state = weights[0] * moments[0:1]
            for n in range(1, WIDE):
                state = state + weights[n] * moments[n : n + 1]
            into[k, :, pl.ds(pl.multiple_of(i * chunk, 128), chunk)] = state
            return carry

        lax.fori_loop(0, slim // chunk, one_chunk, 0)

    def send_slice(k, carry):
        one_slice(k, local_send)
        local_copy(k).start()
        return carry

    lax.fori_loop(1, TEAM, send_slice, 0)
    one_slice(0, local_land)

    def out_copy(k):
        return pltpu.make_async_copy(drive_ref.at[:, span(k)], total_ref.at[:, span(k)], out_sem.at[k])

    def filter_slice(k, carry):
        base = (rank + k) % TEAM * slim

        def one_chunk(i, carry):
            here = pl.ds(pl.multiple_of(base + i * chunk, 128), chunk)
            rate = rate_ref[:, here]
            scale = residue_ref[:, here] * jnp.sqrt(1.0 - jnp.exp(-2.0 * rate))
            scale = scale * jnp.exp(F32(-MIDDLE) * rate)
            close = [jnp.sum(w * scale, axis=0, keepdims=True) for w in lagrange(rate, nodes_of(NEAR))]
            share = jnp.concatenate(
                [jnp.sum(weight_ref[n, :, here], axis=0, keepdims=True) for n in range(WIDE)], axis=0
            )
            skip = skip_ref[:, here]
            moments = product_of(gather_m[...], drive_ref[:, here].astype(BF16))
            moments = moments[:groups] + moments[groups:]
            moments = (moments.reshape(-1, WIDE, chunk) * share[None]).reshape(groups, chunk)
            high, low = halves(moments)
            for b in range(rows // BLOCK):
                span_b = slice(b * BLOCK, (b + 1) * BLOCK)
                drive = drive_ref[span_b, here]
                parts = [(c * drive).astype(BF16) for c in close]
                if b > 0:
                    before = slice((b - 1) * WIDE, b * WIDE)
                    parts += [high[before], high[before], low[before]]
                    weights = block_m[span_b, :]
                else:
                    weights = block_m[span_b, : NEAR * BLOCK]
                drive_ref[span_b, here] = skip * drive + product_of(weights, jnp.concatenate(parts, axis=0))
            return carry

        lax.fori_loop(0, slim // chunk, one_chunk, 0)
        out_copy(k).start()
        return carry

    lax.fori_loop(0, 2, filter_slice, 0)

    mine = pl.ds(pl.multiple_of(rank * slim, 128), slim)
    rate = rate_ref[:, mine]
    fade = jnp.exp(-rate * F32(rows))
    fade_team = jnp.exp(-rate * F32(rows * TEAM))

    def whole(first, devices):
        start = first * rows
        kept = seg_of(start + devices * rows - 1, zero_bounds) == seg_of(start - 1, zero_bounds)
        return kept.astype(F32)

    for k in range(1, TEAM):
        local_copy(k).wait()
    local = [local_land[(rank + TEAM - s) % TEAM] for s in range(TEAM)]
    total = local[0]
    for s in range(1, TEAM):
        total = total * (fade * whole(team * TEAM + s, 1)) + local[s]
    total_land[0] = total

    def total_copy(k):
        return remote(total_land.at[0], total_land.at[k], (total_sem.at[k, 0], total_sem.at[k, 1]), peer(k))

    for k in range(1, teams):
        total_copy(k).start()
    lax.fori_loop(2, 5, filter_slice, 0)
    for k in range(1, teams):
        total_copy(k).wait()
    state = jnp.zeros(rate.shape, F32)
    for g in range(teams - 1):
        after = state * (fade_team * whole(g * TEAM, TEAM)) + total_land[(team + teams - g) % teams]
        state = jnp.where(g < team, after, state)
    for s in range(TEAM):
        back_send[s] = state
        if s < TEAM - 1:
            state = state * (fade * whole(team * TEAM + s, 1)) + local[s]

    def back_copy(k):
        return remote(back_send.at[(rank + k) % TEAM], back_land.at[k], (back_sem.at[k, 0], back_sem.at[k, 1]), mate(k))

    for k in range(1, TEAM):
        back_copy(k).start()
    arrived_ref[:, mine] = back_send[rank]
    lax.fori_loop(5, TEAM, filter_slice, 0)
    for k in range(1, TEAM):
        back_copy(k).wait()
    for k in range(1, TEAM):
        arrived_ref[:, span(TEAM - k)] = back_land[k]

    def entry_chunk(i, carry):
        here = pl.ds(pl.multiple_of(i * chunk, 128), chunk)
        arrived = arrived_ref[:, here]
        entry_ref[:, here] = jnp.concatenate(
            [jnp.sum(weight_ref[n, :, here] * arrived, axis=0, keepdims=True) for n in range(WIDE)], axis=0
        )
        return carry

    lax.fori_loop(0, channels // chunk, entry_chunk, 0)
    for k in range(TEAM):
        out_copy(k).wait()


def output_kernel(
    fused,
    lengths_ref,
    query_ref,
    total_ref,
    edge_ref,
    taps_ref,
    gain_ref,
    entry_ref,
    arrive_ref,
    out_ref,
    square_ref,
    shift_ref,
    arrive_m,
    held_ref,
):
    rows, columns = query_ref.shape[1:]
    phase, step = pl.program_id(0), pl.program_id(1)

    @pl.when((phase == 0) & (step == 0))
    def _():
        bounds = bounds_of(lengths_ref, lax.axis_index("ctx") * rows)
        fill_shifts(shift_ref, bounds)
        square_ref[...] = jnp.zeros_like(square_ref)
        place = lax.broadcasted_iota(jnp.int32, (rows, WIDE), 0)
        same = seg_of(place, bounds) == seg_of(jnp.full((rows, WIDE), -1, jnp.int32), bounds)
        high, low = halves(jnp.where(same, arrive_ref[...], 0.0))
        arrive_m[...] = jnp.concatenate([high, low, high], axis=1)

    @pl.when(phase == 0)
    def _():
        chunk = min(CHUNK, columns)

        def one_chunk(index, carry):
            here = pl.ds(pl.multiple_of(index * chunk, 128), chunk)
            high, low = halves(entry_ref[:, here])
            entry = jnp.concatenate([high, high, low], axis=0)
            taps = taps_ref[:, 0, here]
            for b in range(rows // BLOCK):
                span_b = slice(b * BLOCK, (b + 1) * BLOCK)
                if b == 0:
                    block = jnp.concatenate([edge_ref[:, here], query_ref[0, span_b, here]], axis=0)
                else:
                    block = query_ref[0, b * BLOCK - LEAD : (b + 1) * BLOCK, here]
                query = mix(block, taps, shift_ref[2 * b * BLOCK : 2 * (b + 1) * BLOCK, :])
                response = query * (total_ref[span_b, here] + product_of(arrive_m[span_b, :], entry))
                squares = response * response
                part = squares[:, :128]
                for i in range(1, chunk // 128):
                    part = part + squares[:, i * 128 : (i + 1) * 128]
                square_ref[span_b, :] += part
                if fused:
                    held_ref[step, span_b, here] = response
                else:
                    out_ref[span_b, here] = response
            return carry

        lax.fori_loop(0, columns // chunk, one_chunk, 0)

    if fused:

        @pl.when((phase == 1) & (step == 0))
        def _():
            mean = jnp.sum(square_ref[...], axis=1, keepdims=True) / D
            square_ref[...] = jnp.broadcast_to(lax.rsqrt(mean + eps_norm), square_ref.shape)

        @pl.when(phase == 1)
        def _():
            for b in range(rows // BLOCK):
                span_b = slice(b * BLOCK, (b + 1) * BLOCK)
                scale = square_ref[span_b, :]
                for i in range(columns // 128):
                    here = slice(i * 128, (i + 1) * 128)
                    out_ref[span_b, here] = (held_ref[step, span_b, here] * scale * gain_ref[:, here]).astype(BF16)


def shards(features, short_taps, decay_rate, residue, skip_gain, norm_gain, contig_lengths):
    rows, _, channels = features.shape
    count = lax.axis_size("ctx")
    fused = lax.axis_size("chan") == 1
    poles = decay_rate.shape[0]
    planes = jnp.transpose(features, (1, 0, 2))
    columns = min(2048, channels)
    steps = channels // columns
    gather = jnp.asarray(gather_matrix(rows))
    block = jnp.asarray(block_matrix(rows))
    arrive = jnp.asarray(entry_matrix(rows), F32)
    smem = pl.BlockSpec(memory_space=pltpu.SMEM)

    vmem = pl.BlockSpec(memory_space=pltpu.VMEM)
    slim = channels // TEAM
    teams = count // TEAM
    entry, edge, total = pl.pallas_call(
        exchange_kernel,
        in_specs=[smem, pl.BlockSpec(memory_space=pl.ANY)] + [vmem] * 6,
        out_specs=[vmem, vmem, pl.BlockSpec(memory_space=pl.ANY)],
        out_shape=[
            jax.ShapeDtypeStruct((WIDE, channels), F32),
            jax.ShapeDtypeStruct((LEAD, channels), BF16),
            jax.ShapeDtypeStruct((rows, channels), F32),
        ],
        scratch_shapes=[
            pltpu.VMEM(shift_shape(rows), BF16),
            pltpu.VMEM((2 * WIDE, rows), BF16),
            pltpu.VMEM(gather.shape, BF16),
            pltpu.VMEM(block.shape, BF16),
            pltpu.VMEM((rows, channels), F32),
            pltpu.VMEM((WIDE, poles, channels), F32),
            pltpu.VMEM((poles, channels), F32),
            pltpu.VMEM((2, LEAD + rows, channels), BF16),
            pltpu.VMEM((3, 16, channels), BF16),
            pltpu.VMEM((16, channels // 2), BF16),
            pltpu.VMEM((16, channels // 2), BF16),
            pltpu.VMEM((TEAM, poles, slim), F32),
            pltpu.VMEM((TEAM, poles, slim), F32),
            pltpu.VMEM((teams, poles, slim), F32),
            pltpu.VMEM((TEAM, poles, slim), F32),
            pltpu.VMEM((TEAM, poles, slim), F32),
            pltpu.SemaphoreType.DMA((TEAM,)),
            pltpu.SemaphoreType.DMA,
            pltpu.SemaphoreType.DMA((2,)),
            pltpu.SemaphoreType.DMA((TEAM, 2)),
            pltpu.SemaphoreType.DMA((teams, 2)),
            pltpu.SemaphoreType.DMA((TEAM, 2)),
            pltpu.SemaphoreType.DMA((TEAM,)),
        ],
        compiler_params=pltpu.CompilerParams(
            collective_id=0, has_side_effects=True, vmem_limit_bytes=60 << 20
        ),
        name="exchange",
    )(
        contig_lengths,
        planes,
        short_taps,
        decay_rate,
        residue,
        skip_gain.reshape(1, channels),
        gather,
        block,
    )

    def at(phase, j):
        return jnp.where(phase == 0, j, steps - 1)

    def per_block(shape):
        lead = (0,) * (len(shape) - 1)
        return pl.BlockSpec(shape, lambda phase, j: lead + (at(phase, j),))

    def plane_two(i):
        return pl.BlockSpec((1, rows, columns), lambda phase, j: (i, 0, at(phase, j)))

    def still(array):
        return pl.BlockSpec(array.shape, lambda phase, j: (0,) * array.ndim)

    if fused:
        out_map = lambda phase, j: (0, jnp.where(phase == 0, 0, j))
    else:
        out_map = lambda phase, j: (0, j)
    result, squares = pl.pallas_call(
        functools.partial(output_kernel, fused),
        grid=(2 if fused else 1, steps),
        in_specs=[
            smem,
            plane_two(0),
            per_block((rows, columns)),
            per_block((LEAD, columns)),
            per_block((3, 3, columns)),
            pl.BlockSpec((1, columns), lambda phase, j: (0, j)),
            per_block((WIDE, columns)),
            still(arrive),
        ],
        out_specs=[pl.BlockSpec((rows, columns), out_map), pl.BlockSpec((rows, 128), lambda phase, j: (0, 0))],
        out_shape=[
            jax.ShapeDtypeStruct((rows, channels), BF16 if fused else F32),
            jax.ShapeDtypeStruct((rows, 128), F32),
        ],
        scratch_shapes=[
            pltpu.VMEM(shift_shape(rows), BF16),
            pltpu.VMEM((rows, 3 * WIDE), BF16),
            pltpu.VMEM((steps, rows, columns) if fused else (1, 8, 128), F32),
        ],
        compiler_params=pltpu.CompilerParams(vmem_limit_bytes=60 << 20),
        name="output",
    )(contig_lengths, planes, total, edge, short_taps, norm_gain.reshape(1, channels), entry, arrive)
    if fused:
        return result
    mean = lax.psum(jnp.sum(squares, axis=1, keepdims=True), "chan") / D
    return (result * lax.rsqrt(mean + eps_norm) * norm_gain[None, :]).astype(BF16)


def solution(mesh):
    placed = (
        P("ctx", None, "chan"),
        P(None, None, "chan"),
        P(None, "chan"),
        P(None, "chan"),
        P("chan"),
        P("chan"),
        P(),
    )
    return jax.shard_map(
        shards, mesh=mesh, in_specs=placed, out_specs=P("ctx", "chan"), check_vma=False
    )
```
